256 devices in a mesh: prompt: 16 (over y, x_hi, core), resp: 16 (over x_lo, z).
Axes of the slice: x: 4 (x_hi: 2, x_lo: 2; x = x_hi * 2 + x_lo), y: 4, z: 8, core: 2. Of those that a mesh axis runs over, the one named last changes fastest.
Arguments:
- q_prefix: bfloat16 [16, 1024, 1024], P('prompt', 'resp'), may hold values from -40 to 40
- q_resp: bfloat16 [16, 4, 1024, 1024], P('prompt', None, 'resp'), may hold values from -40 to 40
- k_prefix: bfloat16 [16, 1024, 128], P('prompt', 'resp'), may hold values from -6 to 6
- v_prefix: bfloat16 [16, 1024, 128], P('prompt', 'resp'), may hold values from -6 to 6
- k_resp: bfloat16 [16, 4, 1024, 128], P('prompt', None, 'resp'), may hold values from -6 to 6
- v_resp: bfloat16 [16, 4, 1024, 128], P('prompt', None, 'resp'), may hold values from -6 to 6
- dout_prefix: bfloat16 [16, 1024, 1024], P('prompt', 'resp'), may hold values from -144 to 144
- dout_resp: bfloat16 [16, 4, 1024, 1024], P('prompt', None, 'resp'), may hold values from -144 to 144
- lengths: int32 [16, 4], P('prompt'), may hold values from 1 to 1024, as said below
Outputs:
- dq_prefix: bfloat16 [16, 1024, 1024], P('prompt', 'resp')
- dq_resp: bfloat16 [16, 4, 1024, 1024], P('prompt', None, 'resp')
- dk_prefix: float32 [16, 1024, 128], P('prompt', 'resp')
- dv_prefix: float32 [16, 1024, 128], P('prompt', 'resp')
- dk_resp: float32 [16, 4, 1024, 128], P('prompt', None, 'resp')
- dv_resp: float32 [16, 4, 1024, 128], P('prompt', None, 'resp')
The draws below stay inside these ranges and needn't reach their ends.
Inputs may be any that keep to these rules, and one draw needn't show every extreme that they name: `lengths`: some response has exactly 1024 tokens.
All inputs are finite; a program needn't handle non-finite values.
Results may differ from the reference program's by a relative error of at most 0.019.
Values may be sent and summed in bfloat16 or wider, within the bound.
No kernel may reach another device: no remote copies, remote signals or barrier semaphores. Data moves between devices by JAX's collectives and lax.ppermute only.
A program may use at most 64 MiB of HBM per device.

```python
import jax
import jax.numpy as jnp
from jax import lax

HD = 128
HEADS = 8
RESPS = 4
PROMPTS = 16
PREFIX = 1024
RESP_MAX = 1024


def base_keys(key, shape):
    normal_key = jax.random.fold_in(key, 0)
    normal = jnp.clip(jax.random.normal(normal_key, shape, jnp.float32), -6.0, 6.0)
    mixed = normal
    position = jnp.arange(shape[-2])
    target = (position % 97 == 4)[:, None]
    return jnp.where(target, mixed, mixed)


def aligned_queries(key, shape):
    normal_key = jax.random.fold_in(key, 0)
    normal = jnp.clip(jax.random.normal(normal_key, shape, jnp.float32), -6.0, 6.0)
    mixed = normal
    position = jnp.arange(shape[-2])
    target = (position % 97 == 5)[:, None]
    return jnp.where(target, mixed, mixed)


def draw_k_prefix(key, part):
    shared = jax.random.fold_in(key, 11)
    values_out = base_keys(shared, (PROMPTS, PREFIX, HD))
    return values_out.astype(jnp.bfloat16)


def draw_k_resp(key, part):
    shared = jax.random.fold_in(key, 12)
    values_out = base_keys(shared, (PROMPTS, RESPS, RESP_MAX, HD))
    return values_out.astype(jnp.bfloat16)


def draw_q_prefix(key, part):
    own_key = jax.random.fold_in(key, 3)
    values_out = aligned_queries(own_key, (PROMPTS, PREFIX, HEADS * HD))
    return values_out.astype(jnp.bfloat16)


def draw_q_resp(key, part):
    own_key = jax.random.fold_in(key, 4)
    values_out = aligned_queries(own_key, (PROMPTS, RESPS, RESP_MAX, HEADS * HD))
    return values_out.astype(jnp.bfloat16)


def draw_lengths(key, part):
    key = jax.random.fold_in(key, 7)
    cap_key, pick_key, len_key, resp_key = jax.random.split(key, 4)
    caps = jax.random.randint(cap_key, (PROMPTS,), RESP_MAX // 4, RESP_MAX + 1)
    longest = jax.random.randint(pick_key, (), 0, PROMPTS)
    caps = jnp.where(jnp.arange(PROMPTS) == longest, RESP_MAX, caps)
    drawn = jax.random.randint(len_key, (PROMPTS, RESPS), 1, caps[:, None] + 1)
    chosen = jax.random.randint(resp_key, (PROMPTS,), 0, RESPS)
    full = jnp.arange(RESPS)[None, :] == chosen[:, None]
    return jnp.where(full, caps[:, None], drawn).astype(jnp.int32)


def level_of(key, dims, cuts, smallest, top_value):
    factor_of, own = 1.0, jax.random.fold_in(key, 6)
    for axis_at, parts in cuts:
        draws = jnp.exp(jax.random.uniform(jax.random.fold_in(own, axis_at), (parts,), jnp.float32, smallest / len(cuts), top_value / len(cuts)))
        factor_of = factor_of * jnp.repeat(draws, dims[axis_at] // parts).reshape([-1 if axis == axis_at else 1 for axis in range(len(dims))])
    return factor_of


def centred(key, dims, deviation, bound, shards=(), held_as=jnp.bfloat16):
    gain = level_of(key, dims, shards, -0.22, 0.18) if shards else 1.0
    values = jax.random.normal(key, dims, jnp.float32) * deviation * gain
    return jnp.minimum(jnp.maximum(values, -bound), bound).astype(held_as)


def setup_inputs(seed: int = 0) -> dict:
    splits = jax.random.split(jax.random.key(seed), 10)
    q_prefix = draw_q_prefix(jax.random.fold_in(splits[9], 71), 0)
    q_resp = draw_q_resp(jax.random.fold_in(splits[9], 71), 0)
    k_prefix = draw_k_prefix(jax.random.fold_in(splits[9], 71), 0)
    v_prefix = centred(splits[3], (PROMPTS, PREFIX, HD), 1.0, 6.0, ((0, 16), (1, 16)))
    k_resp = draw_k_resp(jax.random.fold_in(splits[9], 71), 0)
    v_resp = centred(splits[5], (PROMPTS, RESPS, RESP_MAX, HD), 1.0, 6.0, ((0, 16), (2, 16)))
    dout_prefix = centred(splits[6], (PROMPTS, PREFIX, HEADS * HD), 24.0, 144.0, ((0, 16), (1, 16)))
    dout_resp = centred(splits[7], (PROMPTS, RESPS, RESP_MAX, HEADS * HD), 24.0, 144.0, ((0, 16), (2, 16)))
    lengths = draw_lengths(jax.random.fold_in(splits[9], 71), 0)
    return dict(q_prefix=q_prefix, q_resp=q_resp, k_prefix=k_prefix, v_prefix=v_prefix, k_resp=k_resp, v_resp=v_resp, dout_prefix=dout_prefix, dout_resp=dout_resp, lengths=lengths)


def block_grads(queries, douts, query_pos, all_keys, all_values, key_pos):
    head_dim = all_keys.shape[1]
    heads = queries.shape[1] // head_dim
    scale = head_dim ** -0.5
    q_flat = queries.reshape(-1, head_dim)
    d_flat = douts.reshape(-1, head_dim)
    row_pos = jnp.repeat(query_pos, heads)
    allowed = key_pos[None, :] <= row_pos[:, None]
    scores = jnp.dot(q_flat, all_keys.T, preferred_element_type=jnp.float32) * scale
    masked = jnp.where(allowed, scores, -1.0e30)
    row_max = jnp.max(masked, axis=1, keepdims=True)
    log_sum = row_max + jnp.log(jnp.sum(jnp.where(allowed, jnp.exp(masked - row_max), 0.0), axis=1, keepdims=True))
    weights = jnp.where(allowed, jnp.exp(scores - log_sum), 0.0)
    grad_probs = jnp.dot(d_flat, all_values.T, preferred_element_type=jnp.float32)
    row_delta = jnp.sum(weights * grad_probs, axis=1, keepdims=True)
    grad_values = jnp.dot(weights.astype(jnp.bfloat16).T, d_flat, preferred_element_type=jnp.float32)
    grad_scores = (weights * (grad_probs - row_delta)).astype(jnp.bfloat16)
    grad_q = jnp.dot(grad_scores, all_keys, preferred_element_type=jnp.float32) * scale
    grad_keys = jnp.dot(grad_scores.T, q_flat, preferred_element_type=jnp.float32) * scale
    return grad_q.reshape(queries.shape), grad_keys, grad_values


def reference(q_prefix, q_resp, k_prefix, v_prefix, k_resp, v_resp, dout_prefix, dout_resp, lengths):
    total = jnp.sum(lengths.astype(jnp.float32))
    token_scale = jnp.float32(PROMPTS * RESPS * RESP_MAX) / (2.0 * total)
    prefix_len = k_prefix.shape[1]
    resp_len = k_resp.shape[2]
    prefix_pos = jnp.arange(prefix_len, dtype=jnp.int32)
    key_pos = jnp.arange(prefix_len + resp_len, dtype=jnp.int32)
    resp_pos = jnp.arange(resp_len, dtype=jnp.int32)

    def one_prompt(items):
        qp, qr, kp, vp, kr, vr, dp, dr, lens = items
        cot_prefix = (dp.astype(jnp.float32) * token_scale).astype(jnp.bfloat16)
        dq_self, dk_self, dv_self = block_grads(qp, cot_prefix, prefix_pos, kp, vp, prefix_pos)

        def one_response(inner):
            queries, douts, keys_own, values_own, length = inner
            is_live = (resp_pos < length)[:, None]
            scaled = (douts.astype(jnp.float32) * token_scale).astype(jnp.bfloat16)
            cot = jnp.where(is_live, scaled, jnp.zeros_like(scaled))
            all_keys = jnp.concatenate([kp, keys_own], axis=0)
            all_values = jnp.concatenate([vp, values_own], axis=0)
            return block_grads(queries, cot, (prefix_len + resp_pos).astype(jnp.int32), all_keys, all_values, key_pos)

        dq_all, dk_all, dv_all = lax.map(one_response, (qr, dr, kr, vr, lens))
        dk_pre = dk_self + jnp.sum(dk_all[:, :prefix_len], axis=0)
        dv_pre = dv_self + jnp.sum(dv_all[:, :prefix_len], axis=0)
        return (dq_self.astype(jnp.bfloat16), dq_all.astype(jnp.bfloat16), dk_pre, dv_pre,
                dk_all[:, prefix_len:], dv_all[:, prefix_len:])

    return lax.map(one_prompt, (q_prefix, q_resp, k_prefix, v_prefix, k_resp, v_resp, dout_prefix, dout_resp, lengths))
```

```python
import functools

import jax
import jax.numpy as jnp
from jax import lax
from jax.experimental import pallas as pl
from jax.experimental.pallas import tpu as pltpu
from jax.sharding import PartitionSpec as P

HD = 128
HEADS = 8
ROWS = 64
CHUNK = ROWS * HEADS
ZN = 8
NEG = -1e30
SCALE = HD**-0.5
LOG2E = 1.4426950408889634
TILE_BLOCKS = 4
TILE = TILE_BLOCKS * ROWS
VMEM = pl.BlockSpec(memory_space=pltpu.VMEM)
SMEM = pl.BlockSpec(memory_space=pltpu.SMEM)
F32 = jnp.float32
BF16 = jnp.bfloat16


def dot_nt(a, b):
    return lax.dot_general(a, b, (((1,), (1,)), ((), ())), preferred_element_type=F32)


def dot_tn(a, b):
    return lax.dot_general(a, b, (((0,), (0,)), ((), ())), preferred_element_type=F32)


def dot_nn(a, b):
    return lax.dot_general(a, b, (((1,), (0,)), ((), ())), preferred_element_type=F32)


def stack_heads(rows):
    return jnp.concatenate([rows[:, h * HD : (h + 1) * HD] for h in range(HEADS)], axis=0)


def unstack_heads(rows):
    return jnp.concatenate([rows[h * ROWS : (h + 1) * ROWS] for h in range(HEADS)], axis=1)


def keep_mask(key_first, row_first, tile):
    key_pos = key_first + lax.broadcasted_iota(jnp.int32, (tile, CHUNK), 0)
    row_pos = row_first + (lax.broadcasted_iota(jnp.int32, (tile, CHUNK), 1) & (ROWS - 1))
    return key_pos <= row_pos


def stats_step(stats, q, d, kt, vt, keep):
    top, total, mixed = stats
    s = dot_nt(kt, q) * (SCALE * LOG2E)
    g = dot_nt(vt, d)
    if keep is not None:
        s = jnp.where(keep, s, NEG)
    new_top = jnp.maximum(top, jnp.max(s, axis=0, keepdims=True))
    e = jnp.exp2(s - new_top)
    fix = jnp.exp2(top - new_top)
    total = total * fix + jnp.sum(e, axis=0, keepdims=True)
    mixed = mixed * fix + jnp.sum(e * g, axis=0, keepdims=True)
    return new_top, total, mixed


def grads_step(q, d, kt, vt, log_sum, delta, keep):
    s = dot_nt(kt, q) * (SCALE * LOG2E)
    g = dot_nt(vt, d)
    w = jnp.exp2(s - log_sum)
    if keep is not None:
        w = jnp.where(keep, w, 0.0)
    grad_s = (w * (g - delta)).astype(BF16)
    dv = dot_nn(w.astype(BF16), d)
    dk = dot_nn(grad_s, q)
    dq = dot_tn(grad_s, kt)
    return dq, dk, dv


def empty_stats():
    return (
        jnp.full((1, CHUNK), NEG, F32),
        jnp.zeros((1, CHUNK), F32),
        jnp.zeros((1, CHUNK), F32),
    )


def finish(stats):
    top, total, mixed = stats
    return top + jnp.log2(total), mixed / total


def tile_of(ref, lead, first, kind):
    return ref[lead, pl.ds(first, TILE_BLOCKS), kind].reshape(TILE, HD)


def chunk_first(info, chunk):
    half = info[0] ^ (chunk & 1)
    return (half * ZN + info[1]) * ROWS


def chunk_length(info, chunk):
    return info[2 + (chunk >> 1)]


def prefix_kernel(
    info, qr, dr, got, qp, dp, kv_own, kv_pair,
    q_st, d_st, stats_out, dq_out, acc, kv, q1, d1, dq_acc,
):
    half = info[0]
    z = info[1]
    kv[half] = kv_own[...]
    kv[1 - half] = kv_pair[...]
    acc[...] = jnp.zeros_like(acc)
    q1[...] = stack_heads(qp[0])
    d1[...] = stack_heads(dp[0])
    dq_acc[...] = jnp.zeros_like(dq_acc)
    block = half * ZN + z
    tiles = block // TILE_BLOCKS + 1

    def load(tile):
        lead = tile // 2
        first = (tile % 2) * TILE_BLOCKS
        keep = keep_mask(tile * TILE, block * ROWS, TILE)
        return lead, first, keep

    def first_pass(tile, stats):
        lead, first, keep = load(tile)
        return stats_step(
            stats, q1[...], d1[...], tile_of(kv, lead, first, 0), tile_of(kv, lead, first, 1), keep
        )

    log_sum, delta = finish(lax.fori_loop(0, tiles, first_pass, empty_stats()))

    def second_pass(tile, carried):
        lead, first, keep = load(tile)
        dq, dk, dv = grads_step(
            q1[...], d1[...], tile_of(kv, lead, first, 0), tile_of(kv, lead, first, 1),
            log_sum, delta, keep,
        )
        dq_acc[...] += dq
        acc[lead, pl.ds(first, TILE_BLOCKS), 0] += dk.reshape(TILE_BLOCKS, ROWS, HD)
        acc[lead, pl.ds(first, TILE_BLOCKS), 1] += dv.reshape(TILE_BLOCKS, ROWS, HD)
        return carried

    lax.fori_loop(0, tiles, second_pass, 0)
    dq_out[...] = unstack_heads(dq_acc[...])
    for chunk in range(4):
        resp = chunk >> 1
        if chunk & 1:
            queries, douts = got[0, resp], got[1, resp]
        else:
            queries, douts = qr[0, 2 * half + resp], dr[0, 2 * half + resp]
        pos = chunk_first(info, chunk) + lax.broadcasted_iota(jnp.int32, douts.shape, 0)
        douts = jnp.where(pos < chunk_length(info, chunk), douts.astype(F32), 0.0).astype(BF16)
        q_st[chunk] = stack_heads(queries)
        d_st[chunk] = stack_heads(douts)

    def one_chunk(chunk, carried):
        @pl.when(chunk_first(info, chunk) < chunk_length(info, chunk))
        def _():
            stats = empty_stats()
            for lead in range(2):
                for first in range(0, ZN, TILE_BLOCKS):
                    stats = stats_step(
                        stats, q_st[chunk], d_st[chunk],
                        tile_of(kv, lead, first, 0), tile_of(kv, lead, first, 1), None,
                    )
            for row in range(3):
                stats_out[chunk, row : row + 1] = stats[row]

        return carried

    lax.fori_loop(0, 4, one_chunk, 0)


def resp_kernel(info, q_st, d_st, stats_in, kv, log_out, dq_out, grads, acc):
    half = info[0]
    acc[...] = jnp.zeros_like(acc)
    dq_out[...] = jnp.zeros_like(dq_out)

    def one_chunk(chunk, carried):
        @pl.when(chunk_first(info, chunk) < chunk_length(info, chunk))
        def _():
            resp = chunk >> 1
            row_first = chunk_first(info, chunk)
            tiles = row_first // TILE + 1

            def load(tile):
                slot = (tile // 2) ^ half
                first = (tile % 2) * TILE_BLOCKS
                keys = kv[pl.ds(first, TILE_BLOCKS), slot, 0, resp].reshape(TILE, HD)
                values = kv[pl.ds(first, TILE_BLOCKS), slot, 1, resp].reshape(TILE, HD)
                return slot, first, keys, values, keep_mask(tile * TILE, row_first, TILE)

            def first_pass(tile, stats):
                slot, first, keys, values, keep = load(tile)
                return stats_step(stats, q_st[chunk], d_st[chunk], keys, values, keep)

            begin = tuple(stats_in[chunk, row : row + 1] for row in range(3))
            log_sum, delta = finish(lax.fori_loop(0, tiles, first_pass, begin))
            log_out[chunk, 0:1] = log_sum
            log_out[chunk, 1:2] = delta

            def second_pass(tile, inner):
                slot, first, keys, values, keep = load(tile)
                dq, dk, dv = grads_step(
                    q_st[chunk], d_st[chunk], keys, values, log_sum, delta, keep
                )
                dq_out[chunk] += dq
                acc[pl.ds(first, TILE_BLOCKS), slot, 0, resp] += dk.reshape(TILE_BLOCKS, ROWS, HD)
                acc[pl.ds(first, TILE_BLOCKS), slot, 1, resp] += dv.reshape(TILE_BLOCKS, ROWS, HD)
                return inner

            lax.fori_loop(0, tiles, second_pass, 0)

        return carried

    lax.fori_loop(0, 4, one_chunk, 0)
    grads[...] = acc[...].astype(BF16)


def final_kernel(
    info, token_scale, q_st, d_st, logs, dq_in, dqp_in, kv_own, kv_pair, acc_in,
    dqp_out, dq_own, dq_pair, g_own, g_pair, dq_acc, acc,
):
    half = info[0]
    factor = token_scale[0] * SCALE
    dqp_out[0] = (dqp_in[...] * factor).astype(BF16)
    acc[0] = acc_in[half]
    acc[1] = acc_in[1 - half]
    dq_acc[...] = dq_in[...]

    def one_chunk(chunk, carried):
        @pl.when(chunk_first(info, chunk) < chunk_length(info, chunk))
        def _():
            log_sum = logs[chunk, 0:1]
            delta = logs[chunk, 1:2]
            for lead, kv in enumerate((kv_own, kv_pair)):
                for first in range(0, ZN, TILE_BLOCKS):
                    keys = kv[pl.ds(first, TILE_BLOCKS), 0].reshape(TILE, HD)
                    values = kv[pl.ds(first, TILE_BLOCKS), 1].reshape(TILE, HD)
                    dq, dk, dv = grads_step(
                        q_st[chunk], d_st[chunk], keys, values, log_sum, delta, None
                    )
                    dq_acc[chunk] += dq
                    acc[lead, pl.ds(first, TILE_BLOCKS), 0] += dk.reshape(TILE_BLOCKS, ROWS, HD)
                    acc[lead, pl.ds(first, TILE_BLOCKS), 1] += dv.reshape(TILE_BLOCKS, ROWS, HD)

        return carried

    lax.fori_loop(0, 4, one_chunk, 0)
    for resp in range(2):
        dq_own[resp] = unstack_heads((dq_acc[2 * resp] * factor).astype(BF16))
        dq_pair[resp] = unstack_heads((dq_acc[2 * resp + 1] * factor).astype(BF16))
    g_own[...] = acc[0]
    g_pair[...] = acc[1].astype(BF16)


def shape(dims, dtype):
    return jax.ShapeDtypeStruct(dims, dtype)


def call(kernel, ins, outs, scratch, flops, smem):
    return pl.pallas_call(
        kernel,
        out_shape=outs,
        in_specs=[SMEM] * smem + [VMEM] * (ins - smem),
        out_specs=[VMEM] * len(outs),
        scratch_shapes=scratch,
        cost_estimate=pl.CostEstimate(flops=flops, bytes_accessed=4 << 20, transcendentals=0),
        compiler_params=pltpu.CompilerParams(vmem_limit_bytes=48 << 20),
    )


def per_device(
    q_prefix, q_resp, k_prefix, v_prefix, k_resp, v_resp, dout_prefix, dout_resp, lengths
):
    me = lax.axis_index("resp")
    half, z = me // ZN, me % ZN
    pair = [(i, (i + ZN) % (2 * ZN)) for i in range(2 * ZN)]
    columns = [list(range(ZN)), list(range(ZN, 2 * ZN))]

    def swap(value):
        return lax.ppermute(value, "resp", pair)

    def spread(value):
        return lax.all_to_all(value, "resp", 0, 0, axis_index_groups=columns)

    def mine(value):
        return lax.dynamic_slice_in_dim(value, 2 * half, 2, 0)

    def theirs(value):
        return lax.dynamic_slice_in_dim(value, 2 * (1 - half), 2, 0)

    pre = jnp.stack([k_prefix[0], v_prefix[0]])
    kvp_own = spread(jnp.broadcast_to(pre[None], (ZN,) + pre.shape))
    kv_sent = jnp.stack([theirs(k_resp[0]), theirs(v_resp[0])])
    kv_got = swap(kv_sent)
    kv_mine = jnp.stack([mine(k_resp[0]), mine(v_resp[0])])
    block = jnp.stack([kv_mine, kv_got])
    got = swap(jnp.stack([theirs(q_resp[0]), theirs(dout_resp[0])]))
    kvr = spread(jnp.broadcast_to(block[None], (ZN,) + block.shape))
    kvp_pair = swap(kvp_own)

    count = jnp.sum(lengths[0].astype(F32))
    count = jnp.broadcast_to(count, (8, HD))
    for step in (1, 2, 4, 8):
        count = count + lax.ppermute(count, "prompt", [(i, i ^ step) for i in range(16)])
    token_scale = (F32(65536.0) / (2.0 * count[0, :1]))

    info = jnp.concatenate([jnp.stack([half, z]).astype(jnp.int32), mine(lengths[0])])
    st = shape((4, CHUNK, HD), BF16)
    q_st, d_st, stats, dqp, acc_p = call(
        prefix_kernel, 8,
        [st, st, shape((4, 8, CHUNK), F32), shape((ROWS, HEADS * HD), F32),
         shape((2, ZN, 2, ROWS, HD), F32)],
        [pltpu.VMEM((2, ZN, 2, ROWS, HD), BF16), pltpu.VMEM((CHUNK, HD), BF16),
         pltpu.VMEM((CHUNK, HD), BF16), pltpu.VMEM((CHUNK, HD), F32)],
        3 << 30, 1,
    )(info, q_resp, dout_resp, got, q_prefix, dout_prefix, kvp_own, kvp_pair)
    logs, dq_part, grads_r = call(
        resp_kernel, 5,
        [shape((4, 8, CHUNK), F32), shape((4, CHUNK, HD), F32),
         shape((ZN, 2, 2, 2, ROWS, HD), BF16)],
        [pltpu.VMEM((ZN, 2, 2, 2, ROWS, HD), F32)],
        3 << 30, 1,
    )(info, q_st, d_st, stats, kvr)
    terms_r = spread(grads_r)
    dqp_out, dq_own, dq_pair, g_own, g_pair = call(
        final_kernel, 10,
        [shape((1, ROWS, HEADS * HD), BF16), shape((2, ROWS, HEADS * HD), BF16),
         shape((2, ROWS, HEADS * HD), BF16), shape((ZN, 2, ROWS, HD), F32),
         shape((ZN, 2, ROWS, HD), BF16)],
        [pltpu.VMEM((4, CHUNK, HD), F32), pltpu.VMEM((2, ZN, 2, ROWS, HD), F32)],
        4 << 30, 2,
    )(info, token_scale, q_st, d_st, logs, dq_part, dqp, kvp_own, kvp_pair, acc_p)

    g_sum = (g_own + swap(g_pair).astype(F32)).astype(BF16)
    dq_got = swap(dq_pair)
    terms_p = spread(g_sum)
    kinds = jnp.stack([token_scale * F32(SCALE), token_scale])[:, :, None]
    sum_p = jnp.sum(terms_p.astype(F32), axis=0) * kinds
    sum_r = jnp.sum(terms_r.astype(F32), axis=0) * kinds[None, :, :, :, None]
    back = swap(sum_r[1].astype(BF16)).astype(F32)
    first_half = half == 0

    def arrange(own, other):
        return jnp.where(
            first_half, jnp.concatenate([own, other]), jnp.concatenate([other, own])
        )[None]

    return (
        dqp_out,
        arrange(dq_own, dq_got),
        sum_p[0][None],
        sum_p[1][None],
        arrange(sum_r[0, 0], back[0]),
        arrange(sum_r[0, 1], back[1]),
    )


def solution(mesh):
    rows = P("prompt", "resp", None)
    resp_rows = P("prompt", None, "resp", None)
    return jax.shard_map(
        per_device,
        mesh=mesh,
        in_specs=(
            rows, resp_rows, rows, rows, resp_rows, resp_rows, rows, resp_rows, P("prompt", None),
        ),
        out_specs=(rows, resp_rows, rows, rows, resp_rows, resp_rows),
        check_vma=False,
    )
```

```python
import jax
import jax.numpy as jnp
from jax import lax
from jax.experimental import pallas as pl
from jax.experimental.pallas import tpu as pltpu
from jax.sharding import PartitionSpec as P

HD = 128
HEADS = 8
ROWS = 64
CHUNK = ROWS * HEADS
ZN = 8
PROMPTS = 16
TOKENS = 65536.0
DIGIT = 64
KV_ROWS = 512
NEG = -1e30
SCALE = HD**-0.5
LOG2E = 1.4426950408889634
TILE_BLOCKS = 4
TILE = TILE_BLOCKS * ROWS
VMEM = pl.BlockSpec(memory_space=pltpu.VMEM)
SMEM = pl.BlockSpec(memory_space=pltpu.SMEM)
F32 = jnp.float32
BF16 = jnp.bfloat16


def dot_nt(a, b):
    return lax.dot_general(a, b, (((1,), (1,)), ((), ())), preferred_element_type=F32)


def dot_tn(a, b):
    return lax.dot_general(a, b, (((0,), (0,)), ((), ())), preferred_element_type=F32)


def dot_nn(a, b):
    return lax.dot_general(a, b, (((1,), (0,)), ((), ())), preferred_element_type=F32)


def stack_heads(rows):
    return jnp.concatenate([rows[:, h * HD : (h + 1) * HD] for h in range(HEADS)], axis=0)


def unstack_heads(rows):
    return jnp.concatenate([rows[h * ROWS : (h + 1) * ROWS] for h in range(HEADS)], axis=1)


def keep_mask(key_first, row_first, tile):
    key_pos = key_first + lax.broadcasted_iota(jnp.int32, (tile, CHUNK), 0)
    row_pos = row_first + (lax.broadcasted_iota(jnp.int32, (tile, CHUNK), 1) & (ROWS - 1))
    return key_pos <= row_pos


def stats_step(stats, q, d, kt, vt, keep):
    top, total, mixed = stats
    s = dot_nt(kt, q) * (SCALE * LOG2E)
    g = dot_nt(vt, d)
    if keep is not None:
        s = jnp.where(keep, s, NEG)
    new_top = jnp.maximum(top, jnp.max(s, axis=0, keepdims=True))
    e = jnp.exp2(s - new_top)
    fix = jnp.exp2(top - new_top)
    total = total * fix + jnp.sum(e, axis=0, keepdims=True)
    mixed = mixed * fix + jnp.sum(e * g, axis=0, keepdims=True)
    return new_top, total, mixed


def grads_step(q, d, kt, vt, log_sum, delta, keep):
    s = dot_nt(kt, q) * (SCALE * LOG2E)
    g = dot_nt(vt, d)
    w = jnp.exp2(s - log_sum)
    if keep is not None:
        w = jnp.where(keep, w, 0.0)
    grad_s = (w * (g - delta)).astype(BF16)
    dv = dot_nn(w.astype(BF16), d)
    dk = dot_nn(grad_s, q)
    dq = dot_tn(grad_s, kt)
    return dq, dk, dv


def empty_stats():
    return (
        jnp.full((1, CHUNK), NEG, F32),
        jnp.zeros((1, CHUNK), F32),
        jnp.zeros((1, CHUNK), F32),
    )


def finish(stats):
    top, total, mixed = stats
    return top + jnp.log2(total), mixed / total


def tile_of(ref, lead, first, kind):
    return ref[lead, pl.ds(first, TILE_BLOCKS), kind].reshape(TILE, HD)


def chunk_first(info, chunk):
    half = info[0] ^ (chunk & 1)
    return (half * ZN + info[1]) * ROWS


def chunk_length(info, chunk):
    return info[2 + (chunk >> 1)]


def prefix_kernel(
    info, qr, dr, got, qp, dp, kv_own, kv_pair,
    q_st, d_st, stats_out, dq_out, acc, kv, q1, d1, dq_acc,
):
    half = info[0]
    z = info[1]
    kv[half] = kv_own[...]
    kv[1 - half] = kv_pair[...]
    acc[...] = jnp.zeros_like(acc)
    q1[...] = stack_heads(qp[0])
    d1[...] = stack_heads(dp[0])
    dq_acc[...] = jnp.zeros_like(dq_acc)
    block = half * ZN + z
    tiles = block // TILE_BLOCKS + 1

    def load(tile):
        lead = tile // 2
        first = (tile % 2) * TILE_BLOCKS
        keep = keep_mask(tile * TILE, block * ROWS, TILE)
        return lead, first, keep

    def first_pass(tile, stats):
        lead, first, keep = load(tile)
        return stats_step(
            stats, q1[...], d1[...], tile_of(kv, lead, first, 0), tile_of(kv, lead, first, 1), keep
        )

    log_sum, delta = finish(lax.fori_loop(0, tiles, first_pass, empty_stats()))

    def second_pass(tile, carried):
        lead, first, keep = load(tile)
        dq, dk, dv = grads_step(
            q1[...], d1[...], tile_of(kv, lead, first, 0), tile_of(kv, lead, first, 1),
            log_sum, delta, keep,
        )
        dq_acc[...] += dq
        acc[lead, pl.ds(first, TILE_BLOCKS), 0] += dk.reshape(TILE_BLOCKS, ROWS, HD)
        acc[lead, pl.ds(first, TILE_BLOCKS), 1] += dv.reshape(TILE_BLOCKS, ROWS, HD)
        return carried

    lax.fori_loop(0, tiles, second_pass, 0)
    dq_out[...] = unstack_heads(dq_acc[...])
    for chunk in range(4):
        resp = chunk >> 1
        if chunk & 1:
            queries, douts = got[0, resp], got[1, resp]
        else:
            queries, douts = qr[0, 2 * half + resp], dr[0, 2 * half + resp]
        pos = chunk_first(info, chunk) + lax.broadcasted_iota(jnp.int32, douts.shape, 0)
        douts = jnp.where(pos < chunk_length(info, chunk), douts.astype(F32), 0.0).astype(BF16)
        q_st[chunk] = stack_heads(queries)
        d_st[chunk] = stack_heads(douts)

    def one_chunk(chunk, carried):
        @pl.when(chunk_first(info, chunk) < chunk_length(info, chunk))
        def _():
            stats = empty_stats()
            for lead in range(2):
                for first in range(0, ZN, TILE_BLOCKS):
                    stats = stats_step(
                        stats, q_st[chunk], d_st[chunk],
                        tile_of(kv, lead, first, 0), tile_of(kv, lead, first, 1), None,
                    )
            for row in range(3):
                stats_out[chunk, row : row + 1] = stats[row]

        return carried

    lax.fori_loop(0, 4, one_chunk, 0)


def resp_kernel(info, q_st, d_st, stats_in, kv, log_out, dq_out, scale_out, grads, acc):
    half = info[0]
    acc[...] = jnp.zeros_like(acc)
    dq_out[...] = jnp.zeros_like(dq_out)
    counts = jnp.sum(kv[:, KV_ROWS:].astype(F32), axis=0)
    scale_out[...] = TOKENS / (2.0 * (counts[:8] * DIGIT + counts[8:]))

    def one_chunk(chunk, carried):
        @pl.when(chunk_first(info, chunk) < chunk_length(info, chunk))
        def _():
            resp = chunk >> 1
            row_first = chunk_first(info, chunk)
            tiles = row_first // TILE + 1

            def load(tile):
                slot = (tile // 2) ^ half
                first = (tile % 2) * TILE_BLOCKS

                def rows(kind):
                    at = pl.multiple_of(((slot * 2 + kind) * 2 + resp) * ROWS, ROWS)
                    return kv[pl.ds(first, TILE_BLOCKS), pl.ds(at, ROWS)].reshape(TILE, HD)

                return rows(0), rows(1), keep_mask(tile * TILE, row_first, TILE)

            def first_pass(tile, stats):
                keys, values, keep = load(tile)
                return stats_step(stats, q_st[chunk], d_st[chunk], keys, values, keep)

            begin = tuple(stats_in[chunk, row : row + 1] for row in range(3))
            log_sum, delta = finish(lax.fori_loop(0, tiles, first_pass, begin))
            log_out[chunk, 0:1] = log_sum
            log_out[chunk, 1:2] = delta

            def second_pass(tile, inner):
                keys, values, keep = load(tile)
                dq, dk, dv = grads_step(
                    q_st[chunk], d_st[chunk], keys, values, log_sum, delta, keep
                )
                dq_out[chunk] += dq
                at = pl.ds(tile * TILE_BLOCKS, TILE_BLOCKS)
                acc[at, 0, resp] += dk.reshape(TILE_BLOCKS, ROWS, HD)
                acc[at, 1, resp] += dv.reshape(TILE_BLOCKS, ROWS, HD)
                return inner

            lax.fori_loop(0, tiles, second_pass, 0)

        return carried

    lax.fori_loop(0, 4, one_chunk, 0)
    grads[...] = acc[...].astype(BF16)


def half_prefix(info, q_st, d_st, logs, kv, dq_acc, acc):
    def one_chunk(chunk, carried):
        @pl.when(chunk_first(info, chunk) < chunk_length(info, chunk))
        def _():
            log_sum = logs[chunk, 0:1]
            delta = logs[chunk, 1:2]
            for first in range(0, ZN, TILE_BLOCKS):
                keys = kv[pl.ds(first, TILE_BLOCKS), 0].reshape(TILE, HD)
                values = kv[pl.ds(first, TILE_BLOCKS), 1].reshape(TILE, HD)
                dq, dk, dv = grads_step(
                    q_st[chunk], d_st[chunk], keys, values, log_sum, delta, None
                )
                dq_acc[chunk] += dq
                acc[pl.ds(first, TILE_BLOCKS), 0] += dk.reshape(TILE_BLOCKS, ROWS, HD)
                acc[pl.ds(first, TILE_BLOCKS), 1] += dv.reshape(TILE_BLOCKS, ROWS, HD)

        return carried

    lax.fori_loop(0, 4, one_chunk, 0)


def pair_kernel(info, q_st, d_st, logs, dq_in, kv, acc_in, dq_out, g_pair, acc):
    acc[...] = acc_in[1 - info[0]]
    dq_out[...] = dq_in[...]
    half_prefix(info, q_st, d_st, logs, kv, dq_out, acc)
    g_pair[...] = acc[...].astype(BF16)


def own_kernel(
    info, scale, q_st, d_st, logs, dq_in, dqp_in, kv, acc_in,
    dqp_out, dq_own, dq_pair, g_own, dq_acc,
):
    factor = scale[0:1] * SCALE
    wide = jnp.concatenate([factor] * HEADS, axis=1)
    dqp_out[0] = (dqp_in[...] * wide).astype(BF16)
    g_own[...] = acc_in[info[0]]
    dq_acc[...] = dq_in[...]
    half_prefix(info, q_st, d_st, logs, kv, dq_acc, g_own)
    for resp in range(2):
        dq_own[resp] = unstack_heads((dq_acc[2 * resp] * factor).astype(BF16))
        dq_pair[resp] = unstack_heads((dq_acc[2 * resp + 1] * factor).astype(BF16))


def join_kernel(info, g_own, g_got, *outs):
    for step in range(ZN):
        at = (info[1] + step) & (ZN - 1)
        outs[step][...] = (g_own[at] + g_got[at].astype(F32)).astype(outs[step].dtype)


def shape(dims, dtype):
    return jax.ShapeDtypeStruct(dims, dtype)


def call(kernel, kinds, outs, scratch=(), flops=1 << 28, name=None):
    spec = {"s": SMEM, "v": VMEM}
    return pl.pallas_call(
        kernel,
        out_shape=outs,
        in_specs=[spec[kind] for kind in kinds],
        out_specs=[VMEM] * len(outs),
        scratch_shapes=list(scratch),
        name=name,
        cost_estimate=pl.CostEstimate(flops=flops, bytes_accessed=4 << 20, transcendentals=0),
        compiler_params=pltpu.CompilerParams(vmem_limit_bytes=24 << 20),
    )


def per_device(
    q_prefix, q_resp, k_prefix, v_prefix, k_resp, v_resp, dout_prefix, dout_resp, lengths
):
    me = lax.axis_index("resp")
    half, z = me // ZN, me % ZN
    pair = [(i, (i + ZN) % (2 * ZN)) for i in range(2 * ZN)]
    columns = [list(range(ZN)), list(range(ZN, 2 * ZN))]

    def swap(value):
        return lax.ppermute(value, "resp", pair)

    def spread(value):
        return lax.all_to_all(value, "resp", 0, 0, axis_index_groups=columns)

    def mine(value):
        return lax.dynamic_slice_in_dim(value, 2 * half, 2, 0)

    def theirs(value):
        return lax.dynamic_slice_in_dim(value, 2 * (1 - half), 2, 0)

    pre = jnp.stack([k_prefix[0], v_prefix[0]])
    kvp_own = spread(jnp.broadcast_to(pre[None], (ZN,) + pre.shape))
    kvp_pair = swap(kvp_own)

    count = jnp.sum(lengths[0])
    digits = jnp.concatenate(
        [jnp.broadcast_to(count // DIGIT, (8, HD)), jnp.broadcast_to(count % DIGIT, (8, HD))]
    ).astype(BF16)
    counts = None
    for ahead in (0, ZN):
        moves = [
            (p * 2 * ZN + i, ((p - i % ZN - ahead) % PROMPTS) * 2 * ZN + i)
            for p in range(PROMPTS)
            for i in range(2 * ZN)
        ]
        other = lax.ppermute(digits, ("prompt", "resp"), moves)
        counts = other if counts is None else counts + other

    kv_got = swap(jnp.stack([theirs(k_resp[0]), theirs(v_resp[0])]))
    kv_mine = jnp.stack([mine(k_resp[0]), mine(v_resp[0])])
    block = jnp.concatenate([kv_mine.reshape(-1, HD), kv_got.reshape(-1, HD), counts])
    got = swap(jnp.stack([theirs(q_resp[0]), theirs(dout_resp[0])]))
    kvr = spread(jnp.broadcast_to(block[None], (ZN,) + block.shape))

    info = jnp.concatenate([jnp.stack([half, z]).astype(jnp.int32), mine(lengths[0])])
    st = shape((4, CHUNK, HD), BF16)
    part = shape((4, CHUNK, HD), F32)
    half_f32 = shape((ZN, 2, ROWS, HD), F32)
    half_bf16 = shape((ZN, 2, ROWS, HD), BF16)
    rows_bf16 = shape((2, ROWS, HEADS * HD), BF16)
    q_st, d_st, stats, dqp, acc_p = call(
        prefix_kernel, "svvvvvvv",
        [st, st, shape((4, 8, CHUNK), F32), shape((ROWS, HEADS * HD), F32),
         shape((2, ZN, 2, ROWS, HD), F32)],
        [pltpu.VMEM((2, ZN, 2, ROWS, HD), BF16), pltpu.VMEM((CHUNK, HD), BF16),
         pltpu.VMEM((CHUNK, HD), BF16), pltpu.VMEM((CHUNK, HD), F32)],
        5 << 30, "prefix",
    )(info, q_resp, dout_resp, got, q_prefix, dout_prefix, kvp_own, kvp_pair)
    logs, dq_part, scale, grads_r = call(
        resp_kernel, "svvvv",
        [shape((4, 8, CHUNK), F32), part, shape((8, HD), F32),
         shape((2 * ZN, 2, 2, ROWS, HD), BF16)],
        [pltpu.VMEM((2 * ZN, 2, 2, ROWS, HD), F32)],
        5 << 30, "resp",
    )(info, q_st, d_st, stats, kvr)
    terms_r = lax.all_to_all(grads_r, "resp", 0, 0)
    dq_part, g_pair = call(
        pair_kernel, "svvvvvv", [part, half_bf16], [pltpu.VMEM((ZN, 2, ROWS, HD), F32)],
        4 << 30, "pair",
    )(info, q_st, d_st, logs, dq_part, kvp_pair, acc_p)
    g_got = swap(g_pair)
    dqp_out, dq_own, dq_pair, g_own = call(
        own_kernel, "svvvvvvvv",
        [shape((1, ROWS, HEADS * HD), BF16), rows_bf16, rows_bf16, half_f32],
        [pltpu.VMEM((4, CHUNK, HD), F32)],
        4 << 30, "own",
    )(info, scale, q_st, d_st, logs, dq_part, dqp, kvp_own, acc_p)
    dq_got = swap(dq_pair)
    own, *others = call(
        join_kernel, "svv",
        [shape((2, ROWS, HD), F32)] + [shape((2, ROWS, HD), BF16)] * (ZN - 1), name="join",
    )(info, g_own, g_got)
    sum_p = own
    for step, value in enumerate(others, 1):
        moves = [(c + i, c + (i + step) % ZN) for c in (0, ZN) for i in range(ZN)]
        sum_p = sum_p + lax.ppermute(value, "resp", moves).astype(F32)

    row = scale[0:1]
    sum_r = jnp.sum(terms_r.reshape(2, ZN, 2, 2, ROWS, HD).astype(F32), axis=1)
    dq_all = jnp.where(
        half == 0, jnp.concatenate([dq_own, dq_got]), jnp.concatenate([dq_got, dq_own])
    )
    return (
        dqp_out,
        dq_all[None],
        (sum_p[0] * (row * SCALE))[None],
        (sum_p[1] * row)[None],
        (sum_r[:, 0] * (row * SCALE)).reshape(1, 4, ROWS, HD),
        (sum_r[:, 1] * row).reshape(1, 4, ROWS, HD),
    )


def solution(mesh):
    rows = P("prompt", "resp", None)
    resp_rows = P("prompt", None, "resp", None)
    return jax.shard_map(
        per_device,
        mesh=mesh,
        in_specs=(
            rows, resp_rows, rows, rows, resp_rows, resp_rows, rows, resp_rows, P("prompt", None),
        ),
        out_specs=(rows, resp_rows, rows, rows, resp_rows, resp_rows),
        check_vma=False,
    )
```

```python
import jax
import jax.numpy as jnp
from jax import lax
from jax.experimental import pallas as pl
from jax.experimental.pallas import tpu as pltpu
from jax.sharding import PartitionSpec as P

HD = 128
HEADS = 8
ROWS = 64
CHUNK = ROWS * HEADS
ZN = 8
PROMPTS = 16
RESPS = 4
TOKENS = 65536.0
NEG = -1e30
SCALE = HD**-0.5
LOG2E = 1.4426950408889634
TILE_BLOCKS = 4
TILE = TILE_BLOCKS * ROWS
BIG = 24
VMEM = pl.BlockSpec(memory_space=pltpu.VMEM)
SMEM = pl.BlockSpec(memory_space=pltpu.SMEM)
F32 = jnp.float32
BF16 = jnp.bfloat16


def dot_nt(a, b):
    return lax.dot_general(a, b, (((1,), (1,)), ((), ())), preferred_element_type=F32)


def dot_tn(a, b):
    return lax.dot_general(a, b, (((0,), (0,)), ((), ())), preferred_element_type=F32)


def dot_nn(a, b):
    return lax.dot_general(a, b, (((1,), (0,)), ((), ())), preferred_element_type=F32)


def stack_heads(rows):
    return jnp.concatenate([rows[:, h * HD : (h + 1) * HD] for h in range(HEADS)], axis=0)


def unstack_heads(rows):
    return jnp.concatenate([rows[h * ROWS : (h + 1) * ROWS] for h in range(HEADS)], axis=1)


def place():
    me = lax.axis_index("resp")
    return me >> 3, me & (ZN - 1)


def dealt(lengths):
    size = [lengths[0, i] for i in range(RESPS)]
    rank = []
    for i in range(RESPS):
        before = [
            ((size[j] >= size[i]) if j < i else (size[j] > size[i])).astype(jnp.int32)
            for j in range(RESPS)
            if j != i
        ]
        rank.append(before[0] + before[1] + before[2])
    at = [
        sum(jnp.where(rank[i] == k, i, 0) for i in range(1, RESPS)) for k in range(RESPS)
    ]
    return (at[0], at[3]), (at[1], at[2])


def of_half(both, half):
    return tuple(jnp.where(half == 0, a, b) for a, b in zip(*both))


def keep_mask(key_first, row_first, tile):
    key_pos = key_first + lax.broadcasted_iota(jnp.int32, (tile, CHUNK), 0)
    row_pos = row_first + (lax.broadcasted_iota(jnp.int32, (tile, CHUNK), 1) & (ROWS - 1))
    return key_pos <= row_pos


def stats_step(stats, q, d, kt, vt, keep):
    top, total, mixed = stats
    s = dot_nt(kt, q) * (SCALE * LOG2E)
    g = dot_nt(vt, d)
    if keep is not None:
        s = jnp.where(keep, s, NEG)
    new_top = jnp.maximum(top, jnp.max(s, axis=0, keepdims=True))
    e = jnp.exp2(s - new_top)
    fix = jnp.exp2(top - new_top)
    total = total * fix + jnp.sum(e, axis=0, keepdims=True)
    mixed = mixed * fix + jnp.sum(e * g, axis=0, keepdims=True)
    return new_top, total, mixed


def grads_step(q, d, kt, vt, log_sum, delta, keep):
    s = dot_nt(kt, q) * (SCALE * LOG2E)
    g = dot_nt(vt, d)
    w = jnp.exp2(s - log_sum)
    if keep is not None:
        w = jnp.where(keep, w, 0.0)
    grad_s = (w * (g - delta)).astype(BF16)
    dv = dot_nn(w.astype(BF16), d)
    dk = dot_nn(grad_s, q)
    dq = dot_tn(grad_s, kt)
    return dq, dk, dv


def empty_stats():
    return (
        jnp.full((1, CHUNK), NEG, F32),
        jnp.zeros((1, CHUNK), F32),
        jnp.zeros((1, CHUNK), F32),
    )


def finish(stats):
    top, total, mixed = stats
    return top + jnp.log2(total), mixed / total


def chunk_first(chunk):
    half, z = place()
    return ((half ^ (chunk & 1)) * ZN + z) * ROWS


def chunk_length(lengths, chunk):
    first, second = of_half(dealt(lengths), place()[0])
    return lengths[0, jnp.where(chunk < 2, first, second)]


def live_chunks(lengths, body):
    def one(chunk, carried):
        @pl.when(chunk_first(chunk) < chunk_length(lengths, chunk))
        def _():
            body(chunk)

        return carried

    lax.fori_loop(0, 2 * 2, one, 0)


def keys_kernel(lengths, kr, vr, kp, vp, sent, prefix):
    half, _ = place()
    for slot, resp in enumerate(of_half(dealt(lengths), 1 - half)):
        sent[0, slot] = kr[0, resp]
        sent[1, slot] = vr[0, resp]
    for step in range(ZN):
        prefix[step, 0] = kp[0]
        prefix[step, 1] = vp[0]


def pick_kernel(lengths, rows, sent):
    half, _ = place()
    for slot, resp in enumerate(of_half(dealt(lengths), 1 - half)):
        sent[slot] = rows[0, resp]


def block_kernel(lengths, kr, vr, got, _, block, count):
    half, _ = place()
    for slot, resp in enumerate(of_half(dealt(lengths), half)):
        for step in range(ZN):
            block[step, 0, 0, slot] = kr[0, resp]
            block[step, 0, 1, slot] = vr[0, resp]
            block[step, 1, 0, slot] = got[0, slot]
            block[step, 1, 1, slot] = got[1, slot]
    total = lengths[0, 0] + lengths[0, 1] + lengths[0, 2] + lengths[0, 3]
    count[...] = jnp.full(count.shape, total, jnp.int32).astype(F32)


def prefix_kernel(
    lengths, qr, dr, q_got, d_got, qp, dp, kv_own, kv_pair,
    q_st, d_st, stats_out, dq_out, acc, kv, q1, d1, dq_acc,
):
    half, z = place()
    kv[half] = kv_own[...]
    kv[1 - half] = kv_pair[...]
    acc[...] = jnp.zeros_like(acc)
    q1[...] = stack_heads(qp[0])
    d1[...] = stack_heads(dp[0])
    dq_acc[...] = jnp.zeros_like(dq_acc)
    block = half * ZN + z
    tiles = block // TILE_BLOCKS + 1

    def load(tile):
        lead = tile >> 1
        first = (tile & 1) * TILE_BLOCKS
        keys, values = (
            kv[lead, pl.ds(first, TILE_BLOCKS), kind].reshape(TILE, HD) for kind in range(2)
        )
        return lead, first, keys, values, keep_mask(tile * TILE, block * ROWS, TILE)

    def first_pass(tile, stats):
        _, _, keys, values, keep = load(tile)
        return stats_step(stats, q1[...], d1[...], keys, values, keep)

    log_sum, delta = finish(lax.fori_loop(0, tiles, first_pass, empty_stats()))

    def second_pass(tile, carried):
        lead, first, keys, values, keep = load(tile)
        dq, dk, dv = grads_step(q1[...], d1[...], keys, values, log_sum, delta, keep)
        dq_acc[...] += dq
        acc[lead, pl.ds(first, TILE_BLOCKS), 0] += dk.reshape(TILE_BLOCKS, ROWS, HD)
        acc[lead, pl.ds(first, TILE_BLOCKS), 1] += dv.reshape(TILE_BLOCKS, ROWS, HD)
        return carried

    lax.fori_loop(0, tiles, second_pass, 0)
    dq_out[...] = unstack_heads(dq_acc[...])
    responses = of_half(dealt(lengths), half)
    for chunk in range(4):
        slot = chunk >> 1
        if chunk & 1:
            queries, douts = q_got[slot], d_got[slot]
        else:
            queries, douts = qr[0, responses[slot]], dr[0, responses[slot]]
        pos = chunk_first(chunk) + lax.broadcasted_iota(jnp.int32, douts.shape, 0)
        douts = jnp.where(pos < lengths[0, responses[slot]], douts.astype(F32), 0.0).astype(BF16)
        q_st[chunk] = stack_heads(queries)
        d_st[chunk] = stack_heads(douts)

    def body(chunk):
        stats = empty_stats()
        for lead in range(2):
            for first in range(0, ZN, TILE_BLOCKS):
                keys, values = (
                    kv[lead, first : first + TILE_BLOCKS, kind].reshape(TILE, HD)
                    for kind in range(2)
                )
                stats = stats_step(stats, q_st[chunk], d_st[chunk], keys, values, None)
        for row in range(3):
            stats_out[chunk, row : row + 1] = stats[row]

    live_chunks(lengths, body)


def resp_tile(kv, slot, tile):
    half, _ = place()
    which = (tile >> 1) ^ half
    at = pl.ds((tile & 1) * TILE_BLOCKS, TILE_BLOCKS)
    return (kv[at, which, kind, slot].reshape(TILE, HD) for kind in range(2))


def half_prefix(chunk, q_st, d_st, log_sum, delta, kv, dq_acc, acc):
    for first in range(0, ZN, TILE_BLOCKS):
        at = slice(first, first + TILE_BLOCKS)
        keys, values = (kv[at, kind].reshape(TILE, HD) for kind in range(2))
        dq, dk, dv = grads_step(q_st[chunk], d_st[chunk], keys, values, log_sum, delta, None)
        dq_acc[chunk] += dq
        acc[at, 0] += dk.reshape(TILE_BLOCKS, ROWS, HD)
        acc[at, 1] += dv.reshape(TILE_BLOCKS, ROWS, HD)


def resp_kernel(
    lengths, total, q_st, d_st, stats_in, kv, factor_out, log_out, dq_out, grads, acc
):
    factor_out[...] = TOKENS / (2.0 * total[...])
    acc[...] = jnp.zeros_like(acc)
    dq_out[...] = jnp.zeros_like(dq_out)

    def body(chunk):
        row_first = chunk_first(chunk)
        last = row_first // TILE
        slot = chunk >> 1

        def first(tile, stats, keep):
            keys, values = resp_tile(kv, slot, tile)
            return stats_step(stats, q_st[chunk], d_st[chunk], keys, values, keep)

        keep = keep_mask(last * TILE, row_first, TILE)
        stats = tuple(stats_in[chunk, row : row + 1] for row in range(3))
        stats = lax.fori_loop(0, last, lambda tile, now: first(tile, now, None), stats)
        log_sum, delta = finish(first(last, stats, keep))
        log_out[chunk, 0:1] = log_sum
        log_out[chunk, 1:2] = delta

        def second(tile, keep):
            keys, values = resp_tile(kv, slot, tile)
            dq, dk, dv = grads_step(q_st[chunk], d_st[chunk], keys, values, log_sum, delta, keep)
            dq_out[chunk] += dq
            at = pl.ds(tile * TILE_BLOCKS, TILE_BLOCKS)
            acc[at, 0, slot] += dk.reshape(TILE_BLOCKS, ROWS, HD)
            acc[at, 1, slot] += dv.reshape(TILE_BLOCKS, ROWS, HD)

        def plain(tile, carried):
            second(tile, None)
            return carried

        lax.fori_loop(0, last, plain, 0)
        second(last, keep)

    live_chunks(lengths, body)
    grads[...] = acc[...].astype(BF16)


def pair_kernel(lengths, q_st, d_st, logs, dq_in, kv, acc_in, dq_out, g_pair, acc):
    acc[...] = acc_in[1 - place()[0]]
    dq_out[...] = dq_in[...]

    def body(chunk):
        half_prefix(chunk, q_st, d_st, logs[chunk, 0:1], logs[chunk, 1:2], kv, dq_out, acc)

    live_chunks(lengths, body)
    g_pair[...] = acc[...].astype(BF16)


def own_kernel(
    lengths, scale, q_st, d_st, logs, dq_in, dqp_in, kv, acc_in,
    dqp_out, dq_own, dq_pair, g_own, dq_acc,
):
    factor = scale[0:1] * SCALE
    wide = jnp.concatenate([factor] * HEADS, axis=1)
    dqp_out[0] = (dqp_in[...] * wide).astype(BF16)
    g_own[...] = acc_in[place()[0]]
    dq_acc[...] = dq_in[...]

    def body(chunk):
        half_prefix(chunk, q_st, d_st, logs[chunk, 0:1], logs[chunk, 1:2], kv, dq_acc, g_own)

    live_chunks(lengths, body)
    for slot in range(2):
        dq_own[slot] = unstack_heads((dq_acc[2 * slot] * factor).astype(BF16))
        dq_pair[slot] = unstack_heads((dq_acc[2 * slot + 1] * factor).astype(BF16))


def join_kernel(g_own, g_got, *outs):
    _, z = place()
    for step in range(ZN):
        at = (z + step) & (ZN - 1)
        outs[step][...] = (g_own[at] + g_got[at].astype(F32)).astype(outs[step].dtype)


def rows_kernel(lengths, own, got, out):
    half, _ = place()
    both = dealt(lengths)
    for slot, resp in enumerate(of_half(both, half)):
        out[0, resp] = own[slot]
    for slot, resp in enumerate(of_half(both, 1 - half)):
        out[0, resp] = got[slot]


def sums_kernel(lengths, scale, terms, own, *rest):
    others, (dkp, dvp, dkr, dvr) = rest[: ZN - 1], rest[ZN - 1 :]
    factor = scale[0:1]
    for kind, out, by in ((0, dkp, factor * SCALE), (1, dvp, factor)):
        value = own[kind]
        for other in others:
            value = value + other[kind].astype(F32)
        out[0] = value * by
    for half, responses in enumerate(dealt(lengths)):
        for slot, resp in enumerate(responses):
            for kind, out, by in ((0, dkr, factor * SCALE), (1, dvr, factor)):
                value = terms[half * ZN, kind, slot].astype(F32)
                for step in range(1, ZN):
                    value = value + terms[half * ZN + step, kind, slot].astype(F32)
                out[0, resp] = value * by


def shape(dims, dtype):
    return jax.ShapeDtypeStruct(dims, dtype)


def call(kernel, kinds, outs, scratch=(), flops=1 << 20, name=None, vmem=8):
    spec = {"s": SMEM, "v": VMEM, "a": pl.BlockSpec(memory_space=pl.ANY)}
    return pl.pallas_call(
        kernel,
        out_shape=outs,
        in_specs=[spec[kind] for kind in kinds],
        out_specs=[VMEM] * len(outs),
        scratch_shapes=list(scratch),
        name=name,
        cost_estimate=pl.CostEstimate(flops=flops, bytes_accessed=2 << 20, transcendentals=0),
        compiler_params=pltpu.CompilerParams(vmem_limit_bytes=vmem << 20),
    )


def per_device(
    q_prefix, q_resp, k_prefix, v_prefix, k_resp, v_resp, dout_prefix, dout_resp, lengths
):
    pair = [(i, (i + ZN) % (2 * ZN)) for i in range(2 * ZN)]
    columns = [list(range(ZN)), list(range(ZN, 2 * ZN))]

    def swap(value):
        return lax.ppermute(value, "resp", pair)

    def spread(value):
        return lax.all_to_all(value, "resp", 0, 0, axis_index_groups=columns)

    half_f32 = shape((ZN, 2, ROWS, HD), F32)
    half_bf16 = shape((ZN, 2, ROWS, HD), BF16)
    rows_bf16 = shape((2, ROWS, HEADS * HD), BF16)
    st = shape((4, CHUNK, HD), BF16)
    part = shape((4, CHUNK, HD), F32)
    logs_f32 = shape((4, 8, CHUNK), F32)

    kv_sent, prefix = call(
        keys_kernel, "svvvv", [shape((2, 2, ROWS, HD), BF16), half_bf16], name="keys"
    )(lengths, k_resp, v_resp, k_prefix, v_prefix)
    kv_got = swap(kv_sent)
    (q_sent,) = call(pick_kernel, "sv", [rows_bf16], name="queries")(lengths, q_resp)
    q_got = swap(q_sent)
    (d_sent,) = call(pick_kernel, "sv", [rows_bf16], name="douts")(lengths, dout_resp)
    d_got = swap(d_sent)
    kvp_own = spread(prefix)
    kvp_pair = swap(kvp_own)
    block, total = call(
        block_kernel, "svvva",
        [shape((ZN, 2, 2, 2, ROWS, HD), BF16), shape((8, HD), F32)], name="block",
    )(lengths, k_resp, v_resp, kv_got, q_got)
    kvr = spread(block)
    for step in (1, 2, 4, 8):
        total = total + lax.ppermute(total, "prompt", [(i, i ^ step) for i in range(PROMPTS)])

    q_st, d_st, stats, dqp, acc_p = call(
        prefix_kernel, "svvvvvvvv",
        [st, st, logs_f32, shape((ROWS, HEADS * HD), F32), shape((2, ZN, 2, ROWS, HD), F32)],
        [pltpu.VMEM((2, ZN, 2, ROWS, HD), BF16), pltpu.VMEM((CHUNK, HD), BF16),
         pltpu.VMEM((CHUNK, HD), BF16), pltpu.VMEM((CHUNK, HD), F32)],
        5 << 30, "prefix", BIG,
    )(lengths, q_resp, dout_resp, q_got, d_got, q_prefix, dout_prefix, kvp_own, kvp_pair)
    scale, logs, dq_part, grads_r = call(
        resp_kernel, "svvvvv",
        [shape((8, HD), F32), logs_f32, part, shape((2 * ZN, 2, 2, ROWS, HD), BF16)],
        [pltpu.VMEM((2 * ZN, 2, 2, ROWS, HD), F32)], 4 << 30, "resp", BIG,
    )(lengths, total, q_st, d_st, stats, kvr)
    terms_r = lax.all_to_all(grads_r, "resp", 0, 0)
    dq_part, g_pair = call(
        pair_kernel, "svvvvvv", [part, half_bf16],
        [pltpu.VMEM((ZN, 2, ROWS, HD), F32)], 4 << 30, "pair", BIG,
    )(lengths, q_st, d_st, logs, dq_part, kvp_pair, acc_p)
    g_got = swap(g_pair)
    dqp_out, dq_own, dq_pair, g_own = call(
        own_kernel, "svvvvvvvv",
        [shape((1, ROWS, HEADS * HD), BF16), rows_bf16, rows_bf16, half_f32],
        [pltpu.VMEM((4, CHUNK, HD), F32)], 4 << 30, "own", BIG,
    )(lengths, scale, q_st, d_st, logs, dq_part, dqp, kvp_own, acc_p)
    own, *blocks = call(
        join_kernel, "vv",
        [shape((2, ROWS, HD), F32)] + [shape((2, ROWS, HD), BF16)] * (ZN - 1), name="join",
    )(g_own, g_got)
    dq_got = swap(dq_pair)
    others = []
    for step, value in enumerate(blocks, 1):
        moves = [(c + i, c + (i + step) % ZN) for c in (0, ZN) for i in range(ZN)]
        others.append(lax.ppermute(value, "resp", moves))
    (dq_all,) = call(
        rows_kernel, "svv", [shape((1, RESPS, ROWS, HEADS * HD), BF16)], name="rows"
    )(lengths, dq_own, dq_got)
    prefix_out = shape((1, ROWS, HD), F32)
    resp_out = shape((1, RESPS, ROWS, HD), F32)
    dkp, dvp, dkr, dvr = call(
        sums_kernel, "s" + "v" * (ZN + 2), [prefix_out, prefix_out, resp_out, resp_out],
        name="sums",
    )(lengths, scale, terms_r, own, *others)
    return dqp_out, dq_all, dkp, dvp, dkr, dvr


def solution(mesh):
    rows = P("prompt", "resp", None)
    resp_rows = P("prompt", None, "resp", None)
    return jax.shard_map(
        per_device,
        mesh=mesh,
        in_specs=(
            rows, resp_rows, rows, rows, resp_rows, resp_rows, rows, resp_rows, P("prompt", None),
        ),
        out_specs=(rows, resp_rows, rows, rows, resp_rows, resp_rows),
        check_vma=False,
    )
```

```python
import jax
import jax.numpy as jnp
from jax import lax
from jax.experimental import pallas as pl
from jax.experimental.pallas import tpu as pltpu
from jax.sharding import PartitionSpec as P

HD = 128
HEADS = 8
ROWS = 64
CHUNK = ROWS * HEADS
ZN = 8
PROMPTS = 16
RESPS = 4
TOKENS = 65536.0
NEG = -1e30
SCALE = HD**-0.5
LOG2E = 1.4426950408889634
TILE_BLOCKS = 4
TILE = TILE_BLOCKS * ROWS
BIG = 24
HALF_ROWS = 6 * ROWS
COUNT_ROWS = 16
VMEM = pl.BlockSpec(memory_space=pltpu.VMEM)
SMEM = pl.BlockSpec(memory_space=pltpu.SMEM)
F32 = jnp.float32
BF16 = jnp.bfloat16


def dot_nt(a, b):
    return lax.dot_general(a, b, (((1,), (1,)), ((), ())), preferred_element_type=F32)


def dot_tn(a, b):
    return lax.dot_general(a, b, (((0,), (0,)), ((), ())), preferred_element_type=F32)


def dot_nn(a, b):
    return lax.dot_general(a, b, (((1,), (0,)), ((), ())), preferred_element_type=F32)


def stack_heads(rows):
    return jnp.concatenate([rows[:, h * HD : (h + 1) * HD] for h in range(HEADS)], axis=0)


def unstack_heads(rows):
    return jnp.concatenate([rows[h * ROWS : (h + 1) * ROWS] for h in range(HEADS)], axis=1)


def place():
    me = lax.axis_index("resp")
    return me >> 3, me & (ZN - 1)


def dealt(lengths):
    size = [lengths[0, i] for i in range(RESPS)]
    rank = []
    for i in range(RESPS):
        before = [
            ((size[j] >= size[i]) if j < i else (size[j] > size[i])).astype(jnp.int32)
            for j in range(RESPS)
            if j != i
        ]
        rank.append(before[0] + before[1] + before[2])
    at = [
        sum(jnp.where(rank[i] == k, i, 0) for i in range(1, RESPS)) for k in range(RESPS)
    ]
    return (at[0], at[3]), (at[1], at[2])


def of_half(both, half):
    return tuple(jnp.where(half == 0, a, b) for a, b in zip(*both))


def keep_mask(key_first, row_first, tile):
    key_pos = key_first + lax.broadcasted_iota(jnp.int32, (tile, CHUNK), 0)
    row_pos = row_first + (lax.broadcasted_iota(jnp.int32, (tile, CHUNK), 1) & (ROWS - 1))
    return key_pos <= row_pos


def stats_step(stats, q, d, kt, vt, keep):
    top, total, mixed = stats
    s = dot_nt(kt, q) * (SCALE * LOG2E)
    g = dot_nt(vt, d)
    if keep is not None:
        s = jnp.where(keep, s, NEG)
    new_top = jnp.maximum(top, jnp.max(s, axis=0, keepdims=True))
    e = jnp.exp2(s - new_top)
    fix = jnp.exp2(top - new_top)
    total = total * fix + jnp.sum(e, axis=0, keepdims=True)
    mixed = mixed * fix + jnp.sum(e * g, axis=0, keepdims=True)
    return new_top, total, mixed


def grads_step(q, d, kt, vt, log_sum, delta, keep):
    s = dot_nt(kt, q) * (SCALE * LOG2E)
    g = dot_nt(vt, d)
    w = jnp.exp2(s - log_sum)
    if keep is not None:
        w = jnp.where(keep, w, 0.0)
    grad_s = (w * (g - delta)).astype(BF16)
    dv = dot_nn(w.astype(BF16), d)
    dk = dot_nn(grad_s, q)
    dq = dot_tn(grad_s, kt)
    return dq, dk, dv


def empty_stats():
    return (
        jnp.full((1, CHUNK), NEG, F32),
        jnp.zeros((1, CHUNK), F32),
        jnp.zeros((1, CHUNK), F32),
    )


def finish(stats):
    top, total, mixed = stats
    return top + jnp.log2(total), mixed / total


def keys_kernel(lengths, kr, vr, kp, vp, mine, sent, digits):
    half, _ = place()
    both = dealt(lengths)
    for out, responses in ((mine, of_half(both, half)), (sent, of_half(both, 1 - half))):
        rows = [kp[0], vp[0]]
        for resp in responses:
            rows += [kr[0, resp], vr[0, resp]]
        for at, value in enumerate(rows):
            out[at * ROWS : (at + 1) * ROWS] = value
    total = lengths[0, 0] + lengths[0, 1] + lengths[0, 2] + lengths[0, 3]
    upper = lax.broadcasted_iota(jnp.int32, digits.shape, 0) < COUNT_ROWS // 2
    digits[...] = jnp.where(upper, total >> 6, total & 63).astype(F32).astype(BF16)


def block_kernel(mine, got, count_a, count_b, block):
    block[:HALF_ROWS] = mine[...]
    block[HALF_ROWS : 2 * HALF_ROWS] = got[...]
    block[2 * HALF_ROWS :] = (count_a[...].astype(F32) + count_b[...].astype(F32)).astype(BF16)


def queries_kernel(lengths, qr, dr, sent):
    half, _ = place()
    for slot, resp in enumerate(of_half(dealt(lengths), 1 - half)):
        sent[0, slot] = qr[0, resp]
        sent[1, slot] = dr[0, resp]


def tile_at(kv, part, tile):
    at = pl.ds(tile * TILE_BLOCKS, TILE_BLOCKS)
    return [kv[at, part, kind].reshape(TILE, HD) for kind in range(2)]


def main_kernel(lengths, qr, dr, got, qp, dp, *rest):
    blocks, rest = rest[:ZN], rest[ZN:]
    factor_out, dqp_out, dq_own, dq_pair, grads, kv, acc, q1, d1, dq1 = rest
    half, z = place()
    digits = jnp.zeros((COUNT_ROWS, HD), F32)
    for step, block in enumerate(blocks):
        digits = digits + block[2 * HALF_ROWS :].astype(F32)
        for which in range(2):
            at = (half ^ which) * ZN + ((z - step) & (ZN - 1))
            rows = block[which * HALF_ROWS : (which + 1) * HALF_ROWS]
            kv[at] = rows.reshape(3, 2, ROWS, HD)
    total = digits[: COUNT_ROWS // 2] * 64.0 + digits[COUNT_ROWS // 2 :]
    factor = TOKENS / (2.0 * total)
    factor_out[...] = factor
    factor = factor[0:1] * SCALE
    acc[...] = jnp.zeros_like(acc)

    def add(part, tile, keys, values, log_sum, delta, keep):
        dq, dk, dv = grads_step(q1[...], d1[...], keys, values, log_sum, delta, keep)
        dq1[...] += dq
        at = pl.ds(tile * TILE_BLOCKS, TILE_BLOCKS)
        acc[at, part, 0] += dk.reshape(TILE_BLOCKS, ROWS, HD)
        acc[at, part, 1] += dv.reshape(TILE_BLOCKS, ROWS, HD)

    def causal(row_first, part, stats):
        last = row_first // TILE
        keep = keep_mask(last * TILE, row_first, TILE)

        def first(tile, now, keep):
            return stats_step(now, q1[...], d1[...], *tile_at(kv, part, tile), keep)

        stats = lax.fori_loop(0, last, lambda tile, now: first(tile, now, None), stats)
        log_sum, delta = finish(first(last, stats, keep))

        def plain(tile, carried):
            add(part, tile, *tile_at(kv, part, tile), log_sum, delta, None)
            return carried

        lax.fori_loop(0, last, plain, 0)
        add(part, last, *tile_at(kv, part, last), log_sum, delta, keep)
        return log_sum, delta

    q1[...] = stack_heads(qp[0])
    d1[...] = stack_heads(dp[0])
    dq1[...] = jnp.zeros_like(dq1)
    causal((half * ZN + z) * ROWS, 0, empty_stats())
    dqp_out[0] = unstack_heads((dq1[...] * factor).astype(BF16))

    responses = of_half(dealt(lengths), half)
    for slot, resp in enumerate(responses):
        length = lengths[0, resp]
        for which in range(2):
            row_first = ((half ^ which) * ZN + z) * ROWS
            queries, douts = ((qr.at[0, resp], dr.at[0, resp]), (got.at[0, slot], got.at[1, slot]))[which]
            out = (dq_own, dq_pair)[which].at[slot]

            @pl.when(row_first >= length)
            def _():
                out[...] = jnp.zeros_like(out)

            @pl.when(row_first < length)
            def _():
                pos = row_first + lax.broadcasted_iota(jnp.int32, douts.shape, 0)
                live = jnp.where(pos < length, douts[...].astype(F32), 0.0).astype(BF16)
                q1[...] = stack_heads(queries[...])
                d1[...] = stack_heads(live)
                dq1[...] = jnp.zeros_like(dq1)
                stats = empty_stats()
                for tile in range(2 * ZN // TILE_BLOCKS):
                    stats = stats_step(stats, q1[...], d1[...], *tile_at(kv, 0, tile), None)
                log_sum, delta = causal(row_first, 1 + slot, stats)
                for tile in range(2 * ZN // TILE_BLOCKS):
                    add(0, tile, *tile_at(kv, 0, tile), log_sum, delta, None)
                out[...] = unstack_heads((dq1[...] * factor).astype(BF16))

    grads[...] = acc[...].astype(BF16)


def rows_kernel(lengths, own, got, out):
    half, _ = place()
    both = dealt(lengths)
    for slot, resp in enumerate(of_half(both, half)):
        out[0, resp] = own[slot]
    for slot, resp in enumerate(of_half(both, 1 - half)):
        out[0, resp] = got[slot]


def sums_kernel(lengths, scale, terms, dkp, dvp, dkr, dvr):
    def summed(sources, part, kind):
        value = terms[sources[0], part, kind].astype(F32)
        for source in sources[1:]:
            value = value + terms[source, part, kind].astype(F32)
        return value

    factor = scale[0:1]
    for kind, out, by in ((0, dkp, factor * SCALE), (1, dvp, factor)):
        out[0] = summed(range(2 * ZN), 0, kind) * by
    for half, responses in enumerate(dealt(lengths)):
        sources = range(half * ZN, (half + 1) * ZN)
        for slot, resp in enumerate(responses):
            for kind, out, by in ((0, dkr, factor * SCALE), (1, dvr, factor)):
                out[0, resp] = summed(sources, 1 + slot, kind) * by


def shape(dims, dtype):
    return jax.ShapeDtypeStruct(dims, dtype)


def call(kernel, kinds, outs, scratch=(), flops=1 << 20, name=None, vmem=8):
    spec = {"s": SMEM, "v": VMEM, "a": pl.BlockSpec(memory_space=pl.ANY)}
    return pl.pallas_call(
        kernel,
        out_shape=outs,
        in_specs=[spec[kind] for kind in kinds],
        out_specs=[VMEM] * len(outs),
        scratch_shapes=list(scratch),
        name=name,
        cost_estimate=pl.CostEstimate(flops=flops, bytes_accessed=2 << 20, transcendentals=0),
        compiler_params=pltpu.CompilerParams(vmem_limit_bytes=vmem << 20),
    )


def per_device(
    q_prefix, q_resp, k_prefix, v_prefix, k_resp, v_resp, dout_prefix, dout_resp, lengths
):
    pair = [(i, (i + ZN) % (2 * ZN)) for i in range(2 * ZN)]

    def swap(value):
        return lax.ppermute(value, "resp", pair)

    def shift(value, by):
        moves = [(c + i, c + (i + by) % ZN) for c in (0, ZN) for i in range(ZN)]
        return lax.ppermute(value, "resp", moves)

    rows_bf16 = shape((2, ROWS, HEADS * HD), BF16)
    half_keys = shape((HALF_ROWS, HD), BF16)
    mine, sent, digits = call(
        keys_kernel, "svvvv", [half_keys, half_keys, shape((COUNT_ROWS, HD), BF16)],
        name="keys", vmem=60,
    )(lengths, k_resp, v_resp, k_prefix, v_prefix)
    kv_got = swap(sent)
    counts = []
    for ahead in (0, ZN):
        moves = [
            (p * 2 * ZN + i, ((p - i % ZN - ahead) % PROMPTS) * 2 * ZN + i)
            for p in range(PROMPTS)
            for i in range(2 * ZN)
        ]
        counts.append(lax.ppermute(digits, ("prompt", "resp"), moves))
    (q_sent,) = call(
        queries_kernel, "svv", [shape((2, 2, ROWS, HEADS * HD), BF16)], name="queries", vmem=60
    )(lengths, q_resp, dout_resp)
    got = swap(q_sent)
    (block,) = call(
        block_kernel, "vvvv", [shape((2 * HALF_ROWS + COUNT_ROWS, HD), BF16)], name="block"
    )(mine, kv_got, *counts)
    blocks = [block] * ZN
    for step in range(1, ZN // 2 + 1):
        blocks[step] = shift(blocks[step - 1], 1)
        if step < ZN // 2:
            blocks[ZN - step] = shift(blocks[(ZN - step + 1) % ZN], -1)

    terms = shape((2 * ZN, 3, 2, ROWS, HD), BF16)
    scale, dqp_out, dq_own, dq_pair, grads = call(
        main_kernel, "s" + "v" * (ZN + 5),
        [shape((8, HD), F32), shape((1, ROWS, HEADS * HD), BF16), rows_bf16, rows_bf16, terms],
        [pltpu.VMEM((2 * ZN, 3, 2, ROWS, HD), BF16), pltpu.VMEM((2 * ZN, 3, 2, ROWS, HD), F32),
         pltpu.VMEM((CHUNK, HD), BF16), pltpu.VMEM((CHUNK, HD), BF16),
         pltpu.VMEM((CHUNK, HD), F32)],
        9 << 30, "main", BIG,
    )(lengths, q_resp, dout_resp, got, q_prefix, dout_prefix, *blocks)
    terms = lax.all_to_all(grads, "resp", 0, 0)
    dq_got = swap(dq_pair)
    (dq_all,) = call(
        rows_kernel, "svv", [shape((1, RESPS, ROWS, HEADS * HD), BF16)], name="rows"
    )(lengths, dq_own, dq_got)
    prefix_out = shape((1, ROWS, HD), F32)
    resp_out = shape((1, RESPS, ROWS, HD), F32)
    dkp, dvp, dkr, dvr = call(
        sums_kernel, "svv", [prefix_out, prefix_out, resp_out, resp_out],
        name="sums",
    )(lengths, scale, terms)
    return dqp_out, dq_all, dkp, dvp, dkr, dvr


def solution(mesh):
    rows = P("prompt", "resp", None)
    resp_rows = P("prompt", None, "resp", None)
    return jax.shard_map(
        per_device,
        mesh=mesh,
        in_specs=(
            rows, resp_rows, rows, rows, resp_rows, resp_rows, rows, resp_rows, P("prompt", None),
        ),
        out_specs=(rows, resp_rows, rows, rows, resp_rows, resp_rows),
        check_vma=False,
    )
```

```python
import jax
import jax.numpy as jnp
from jax import lax
from jax.experimental import pallas as pl
from jax.experimental.pallas import tpu as pltpu
from jax.sharding import PartitionSpec as P

HD = 128
HEADS = 8
ROWS = 64
CHUNK = ROWS * HEADS
ZN = 8
PROMPTS = 16
RESPS = 4
TOKENS = 65536.0
NEG = -1e30
SCALE = HD**-0.5
LOG2E = 1.4426950408889634
TILE_BLOCKS = 8
TILE = TILE_BLOCKS * ROWS
BIG = 30
HALF_ROWS = 6 * ROWS
VMEM = pl.BlockSpec(memory_space=pltpu.VMEM)
SMEM = pl.BlockSpec(memory_space=pltpu.SMEM)
F32 = jnp.float32
BF16 = jnp.bfloat16


def dot_nt(a, b):
    return lax.dot_general(a, b, (((1,), (1,)), ((), ())), preferred_element_type=F32)


def dot_tn(a, b):
    return lax.dot_general(a, b, (((0,), (0,)), ((), ())), preferred_element_type=F32)


def dot_nn(a, b):
    return lax.dot_general(a, b, (((1,), (0,)), ((), ())), preferred_element_type=F32)


def stack_heads(rows):
    return jnp.concatenate([rows[:, h * HD : (h + 1) * HD] for h in range(HEADS)], axis=0)


def unstack_heads(rows):
    return jnp.concatenate([rows[h * ROWS : (h + 1) * ROWS] for h in range(HEADS)], axis=1)


def place():
    me = lax.axis_index("resp")
    return me >> 3, me & (ZN - 1)


def dealt(lengths):
    size = [lengths[0, i] for i in range(RESPS)]
    rank = []
    for i in range(RESPS):
        before = [
            ((size[j] >= size[i]) if j < i else (size[j] > size[i])).astype(jnp.int32)
            for j in range(RESPS)
            if j != i
        ]
        rank.append(before[0] + before[1] + before[2])
    at = [
        sum(jnp.where(rank[i] == k, i, 0) for i in range(1, RESPS)) for k in range(RESPS)
    ]
    return (at[1], at[2]), (at[0], at[3])


def of_half(both, half):
    return tuple(jnp.where(half == 0, a, b) for a, b in zip(*both))


def fold(value):
    return value.reshape(value.shape[0] // 8, 8, CHUNK)


def half_rows(out, kr, vr, kp, vp, responses):
    rows = [kp[0], vp[0]]
    for resp in responses:
        rows += [kr[0, resp], vr[0, resp]]
    for at, value in enumerate(rows):
        out[at * ROWS : (at + 1) * ROWS] = value


def keys_kernel(lengths, kr, vr, kp, vp, sent, count):
    half, _ = place()
    half_rows(sent, kr, vr, kp, vp, of_half(dealt(lengths), 1 - half))
    total = lengths[0, 0] + lengths[0, 1] + lengths[0, 2] + lengths[0, 3]
    count[...] = jnp.full(count.shape, total, jnp.int32).astype(F32)


def queries_kernel(lengths, qr, dr, qp, dp, own, sent, done):
    half, z = place()
    both = dealt(lengths)
    pos = (half * ZN + z) * ROWS + lax.broadcasted_iota(jnp.int32, (ROWS, HEADS * HD), 0)
    for out, responses in ((own, of_half(both, half)), (sent, of_half(both, 1 - half))):
        for slot, resp in enumerate(responses):
            live = jnp.where(pos < lengths[0, resp], dr[0, resp].astype(F32), 0.0)
            out[0, slot] = stack_heads(qr[0, resp])
            out[1, slot] = stack_heads(live.astype(BF16))
    own[0, 2] = stack_heads(qp[0])
    own[1, 2] = stack_heads(dp[0])
    done[...] = jnp.zeros_like(done)


def block_kernel(lengths, kr, vr, kp, vp, got, _, block):
    half_rows(block, kr, vr, kp, vp, of_half(dealt(lengths), place()[0]))
    block[HALF_ROWS:] = got[...]


def tile_at(kv, part, tile, size=TILE):
    at = pl.ds(tile * TILE_BLOCKS, size // ROWS)
    return [kv[at, part, kind].reshape(size, HD) for kind in range(2)]


def token_factor(total):
    return TOKENS / (2.0 * total[0:1])


def attend(
    tail, z, kv, q_ref, d_ref, part, high, shared, acc, factor,
    dq_out, dq1, kept_s, kept_g,
):
    q, d = q_ref[...], d_ref[...]
    tiles = [(0, 0), (0, 1)] if shared else []
    base = len(tiles)

    def rows_of(place, size):
        return pl.ds(pl.multiple_of(place * TILE, TILE), size)

    def over_tiles(body, now):
        for own, tile in tiles:
            now = body(now, own, tile, tile, TILE, False)
        now = lax.fori_loop(0, high, lambda tile, now: body(now, part, tile, base + tile, TILE, False), now)
        return body(now, part, high, base + high, tail, True)

    def scores(top, part, tile, place, size, masked):
        keys, _ = tile_at(kv, part, tile, size)
        s = dot_nt(keys, q) * (SCALE * LOG2E)
        if masked:
            ahead = lax.broadcasted_iota(jnp.int32, s.shape, 0) - (
                lax.broadcasted_iota(jnp.int32, s.shape, 1) & (ROWS - 1)
            )
            s = jnp.where(ahead <= z * ROWS, s, NEG)
        kept_s[rows_of(place, size)] = s
        return jnp.maximum(top, jnp.max(fold(s), axis=0))

    top = over_tiles(scores, jnp.full((8, CHUNK), NEG, F32))
    top = jnp.max(top, axis=0, keepdims=True)

    def sums(now, part, tile, place, size, masked):
        _, values = tile_at(kv, part, tile, size)
        at = rows_of(place, size)
        g = dot_nt(values, d)
        e = jnp.exp2(kept_s[at] - top)
        kept_s[at] = e
        kept_g[at] = g
        return now[0] + jnp.sum(fold(e), axis=0), now[1] + jnp.sum(fold(e * g), axis=0)

    now = over_tiles(sums, (jnp.zeros((8, CHUNK), F32), jnp.zeros((8, CHUNK), F32)))
    total, mixed = (jnp.sum(value, axis=0, keepdims=True) for value in now)
    inverse = 1.0 / total
    delta = mixed * inverse

    def grads(now, part, tile, place, size, masked):
        keys, _ = tile_at(kv, part, tile, size)
        at = rows_of(place, size)
        w = kept_s[at] * inverse
        grad_s = (w * (kept_g[at] - delta)).astype(BF16)
        dv = dot_nn(w.astype(BF16), d)
        dk = dot_nn(grad_s, q)
        dq1[...] += dot_tn(keys, grad_s)
        at = pl.ds(tile * TILE_BLOCKS, size // ROWS)
        acc[at, part, 0] += dk.reshape(size // ROWS, ROWS, HD)
        acc[at, part, 1] += dv.reshape(size // ROWS, ROWS, HD)
        return now

    dq1[...] = jnp.zeros_like(dq1)
    over_tiles(grads, 0)
    dq_out[...] = (jnp.transpose(dq1[...]) * factor).astype(BF16)


def main_kernel(lengths, total, own, got, *rest):
    blocks, rest = rest[:ZN], rest[ZN:]
    dqp_out, dq_own, dq_pair, rest = rest[0], rest[1], rest[2], rest[3:]
    terms, (kv, acc, q_st, d_st, dq_st, *work) = rest[:ZN], rest[ZN:]
    half, z = place()
    factor = token_factor(total) * SCALE
    for step, block in enumerate(blocks):
        for which in range(2):
            at = (half ^ which) * ZN + ((z - step) & (ZN - 1))
            rows = block[which * HALF_ROWS : (which + 1) * HALF_ROWS]
            kv[at] = rows.reshape(3, 2, ROWS, HD)
    acc[...] = jnp.zeros_like(acc)
    dq_st[...] = jnp.zeros_like(dq_st)
    for slot in range(2):
        for kind, ref in enumerate((q_st, d_st)):
            ref[2 * slot] = own[kind, slot]
            ref[2 * slot + 1] = got[kind, slot]
    first, second = of_half(dealt(lengths), half)

    def all_rows(tail):
        attend(
            tail, z, kv, own.at[0, 2], own.at[1, 2], 0, half, False, acc, factor, dqp_out, *work
        )

        def one(chunk, carried):
            slot = chunk >> 1
            high = half ^ (chunk & 1)

            @pl.when((high * ZN + z) * ROWS < lengths[0, jnp.where(slot == 0, first, second)])
            def _():
                attend(
                    tail, z, kv, q_st.at[chunk], d_st.at[chunk], 1 + slot, high, True, acc,
                    factor, dq_st.at[chunk], *work,
                )

            return carried

        lax.fori_loop(0, 4, one, 0)

    pl.when(z < ZN // 2)(lambda: all_rows(TILE // 2))
    pl.when(z >= ZN // 2)(lambda: all_rows(TILE))
    for slot in range(2):
        dq_own[slot] = dq_st[2 * slot]
        dq_pair[slot] = dq_st[2 * slot + 1]
    for step, out in enumerate(terms):
        for which in range(2):
            at = (half ^ which) * ZN + ((z + step) & (ZN - 1))
            out[which * HALF_ROWS : (which + 1) * HALF_ROWS] = (
                acc[at].reshape(HALF_ROWS, HD).astype(BF16)
            )


def add_kernel(got, term, out):
    out[...] = (got[...].astype(F32) + term[...].astype(F32)).astype(BF16)


def column_kernel(own, up, down, mine, sent):
    total = own[...].astype(F32) + up[...].astype(F32) + down[...].astype(F32)
    mine[...] = total[:HALF_ROWS]
    sent[...] = total[HALF_ROWS:].astype(BF16)


def rows_kernel(lengths, prefix, own, got, prefix_out, out):
    prefix_out[0] = unstack_heads(prefix[...])
    half, _ = place()
    both = dealt(lengths)
    for slot, resp in enumerate(of_half(both, half)):
        out[0, resp] = unstack_heads(own[slot])
    for slot, resp in enumerate(of_half(both, 1 - half)):
        out[0, resp] = unstack_heads(got[slot])


def sums_kernel(lengths, total, mine, got, dkp, dvp, dkr, dvr):
    half, _ = place()
    both = dealt(lengths)
    factor = token_factor(total)
    for kind, outs, by in ((0, (dkp, dkr), factor * SCALE), (1, (dvp, dvr), factor)):
        outs[0][0] = (mine[kind * ROWS : (kind + 1) * ROWS] + got[kind * ROWS : (kind + 1) * ROWS].astype(F32)) * by
        for source, responses in ((mine, of_half(both, half)), (got, of_half(both, 1 - half))):
            for slot, resp in enumerate(responses):
                at = ((1 + slot) * 2 + kind) * ROWS
                outs[1][0, resp] = source[at : at + ROWS].astype(F32) * by


def shape(dims, dtype):
    return jax.ShapeDtypeStruct(dims, dtype)


def call(kernel, kinds, outs, scratch=(), flops=1 << 20, name=None, vmem=8):
    spec = {"s": SMEM, "v": VMEM}
    return pl.pallas_call(
        kernel,
        out_shape=outs,
        in_specs=[spec[kind] for kind in kinds],
        out_specs=[VMEM] * len(outs),
        scratch_shapes=list(scratch),
        name=name,
        cost_estimate=pl.CostEstimate(flops=flops, bytes_accessed=2 << 20, transcendentals=0),
        compiler_params=pltpu.CompilerParams(vmem_limit_bytes=vmem << 20),
    )


def per_device(
    q_prefix, q_resp, k_prefix, v_prefix, k_resp, v_resp, dout_prefix, dout_resp, lengths
):
    pair = [(i, (i + ZN) % (2 * ZN)) for i in range(2 * ZN)]

    def swap(value):
        return lax.ppermute(value, "resp", pair)

    def shift(value, by):
        moves = [(c + i, c + (i + by) % ZN) for c in (0, ZN) for i in range(ZN)]
        return lax.ppermute(value, "resp", moves)

    def add_count(value, step):
        return lax.ppermute(value, "prompt", [(i, i ^ step) for i in range(PROMPTS)])

    count = shape((8, HD), F32)
    half_keys = shape((HALF_ROWS, HD), BF16)
    sent, total = call(
        keys_kernel, "svvvv", [half_keys, count], name="keys", vmem=60
    )(lengths, k_resp, v_resp, k_prefix, v_prefix)
    kv_got = swap(sent)
    own, q_sent, built = call(
        queries_kernel, "svvvv",
        [shape((2, 3, CHUNK, HD), BF16), shape((2, 2, CHUNK, HD), BF16), count],
        name="queries", vmem=24,
    )(lengths, q_resp, dout_resp, q_prefix, dout_prefix)
    got = swap(q_sent)
    (block,) = call(
        block_kernel, "svvvvvv", [shape((2 * HALF_ROWS, HD), BF16)], name="block"
    )(lengths, k_resp, v_resp, k_prefix, v_prefix, kv_got, built)
    blocks = [block] * ZN
    for step in range(1, ZN // 2 + 1):
        before = blocks[step - 1]
        if step > 1:
            total = total + add_count(total, (2, 1, 4)[step - 2])
            before, total = lax.optimization_barrier((before, total))
        blocks[step] = shift(before, 1)
        if step < ZN // 2:
            blocks[ZN - step] = shift(blocks[(ZN - step + 1) % ZN], -1)
    total = total + add_count(total, 8)
    rows = shape((2, CHUNK, HD), BF16)
    dqp, dq_own, dq_pair, *terms = call(
        main_kernel, "s" + "v" * (ZN + 3),
        [shape((CHUNK, HD), BF16), rows, rows] + [shape((2 * HALF_ROWS, HD), BF16)] * ZN,
        [pltpu.VMEM((2 * ZN, 3, 2, ROWS, HD), BF16), pltpu.VMEM((2 * ZN, 3, 2, ROWS, HD), F32),
         pltpu.VMEM((4, CHUNK, HD), BF16), pltpu.VMEM((4, CHUNK, HD), BF16),
         pltpu.VMEM((4, CHUNK, HD), BF16), pltpu.VMEM((HD, CHUNK), F32),
         pltpu.VMEM((4 * TILE, CHUNK), F32), pltpu.VMEM((4 * TILE, CHUNK), F32)],
        9 << 30, "main", BIG,
    )(lengths, total, own, got, *blocks)

    def add(got, term):
        return call(add_kernel, "vv", [shape((2 * HALF_ROWS, HD), BF16)], name="add")(got, term)[0]

    up, down = terms[ZN // 2], terms[ZN // 2 + 1]
    for step in range(ZN // 2 - 1, 0, -1):
        up = add(shift(up, 1), terms[step])
        if step > 1:
            down = add(shift(down, -1), terms[ZN - step + 1])
    mine, sent = call(column_kernel, "vvv", [shape((HALF_ROWS, HD), F32), half_keys], name="column")(
        terms[0], shift(up, 1), shift(down, -1)
    )
    terms_got = swap(sent)
    dq_got = swap(dq_pair)
    dqp_out, dq_all = call(
        rows_kernel, "svvv",
        [shape((1, ROWS, HEADS * HD), BF16), shape((1, RESPS, ROWS, HEADS * HD), BF16)],
        name="rows",
    )(lengths, dqp, dq_own, dq_got)
    prefix_out = shape((1, ROWS, HD), F32)
    resp_out = shape((1, RESPS, ROWS, HD), F32)
    dkp, dvp, dkr, dvr = call(
        sums_kernel, "svvv", [prefix_out, prefix_out, resp_out, resp_out],
        name="sums",
    )(lengths, total, mine, terms_got)
    return dqp_out, dq_all, dkp, dvp, dkr, dvr


def solution(mesh):
    rows = P("prompt", "resp", None)
    resp_rows = P("prompt", None, "resp", None)
    return jax.shard_map(
        per_device,
        mesh=mesh,
        in_specs=(
            rows, resp_rows, rows, rows, resp_rows, resp_rows, rows, resp_rows, P("prompt", None),
        ),
        out_specs=(rows, resp_rows, rows, rows, resp_rows, resp_rows),
        check_vma=False,
    )
```

```python
import functools

import jax
import jax.numpy as jnp
from jax import lax
from jax.experimental import pallas as pl
from jax.experimental.pallas import tpu as pltpu
from jax.sharding import PartitionSpec as P

HD = 128
HEADS = 8
ROWS = 64
CHUNK = ROWS * HEADS
ZN = 8
PROMPTS = 16
RESPS = 4
TOKENS = 65536.0
NEG = -1e30
SCALE = HD**-0.5
LOG2E = 1.4426950408889634
TILE_BLOCKS = 8
TILE = TILE_BLOCKS * ROWS
BIG = 30
HALF_ROWS = 6 * ROWS
VMEM = pl.BlockSpec(memory_space=pltpu.VMEM)
SMEM = pl.BlockSpec(memory_space=pltpu.SMEM)
F32 = jnp.float32
BF16 = jnp.bfloat16


def dot_nt(a, b):
    return lax.dot_general(a, b, (((1,), (1,)), ((), ())), preferred_element_type=F32)


def dot_tn(a, b):
    return lax.dot_general(a, b, (((0,), (0,)), ((), ())), preferred_element_type=F32)


def dot_nn(a, b):
    return lax.dot_general(a, b, (((1,), (0,)), ((), ())), preferred_element_type=F32)


def stack_heads(rows):
    return jnp.concatenate([rows[:, h * HD : (h + 1) * HD] for h in range(HEADS)], axis=0)


def unstack_heads(rows):
    return jnp.concatenate([rows[h * ROWS : (h + 1) * ROWS] for h in range(HEADS)], axis=1)


def place():
    me = lax.axis_index("resp")
    return me >> 3, me & (ZN - 1)


def dealt(lengths):
    size = [lengths[0, i] for i in range(RESPS)]
    rank = []
    for i in range(RESPS):
        before = [
            ((size[j] >= size[i]) if j < i else (size[j] > size[i])).astype(jnp.int32)
            for j in range(RESPS)
            if j != i
        ]
        rank.append(before[0] + before[1] + before[2])
    at = [
        sum(jnp.where(rank[i] == k, i, 0) for i in range(1, RESPS)) for k in range(RESPS)
    ]
    return (at[1], at[2]), (at[0], at[3])


def of_half(both, half):
    return tuple(jnp.where(half == 0, a, b) for a, b in zip(*both))


def fold(value):
    return value.reshape(value.shape[0] // 8, 8, CHUNK)


def half_rows(out, kr, vr, kp, vp, responses):
    rows = [kp[0], vp[0]]
    for resp in responses:
        rows += [kr[0, resp], vr[0, resp]]
    for at, value in enumerate(rows):
        out[at * ROWS : (at + 1) * ROWS] = value


def keys_kernel(lengths, kr, vr, kp, vp, sent, count):
    half, _ = place()
    half_rows(sent, kr, vr, kp, vp, of_half(dealt(lengths), 1 - half))
    total = lengths[0, 0] + lengths[0, 1] + lengths[0, 2] + lengths[0, 3]
    count[...] = jnp.full(count.shape, total, jnp.int32).astype(F32)


def queries_kernel(lengths, qr, dr, qp, dp, own, sent, done):
    half, z = place()
    both = dealt(lengths)
    pos = (half * ZN + z) * ROWS + lax.broadcasted_iota(jnp.int32, (ROWS, HEADS * HD), 0)
    for out, responses in ((own, of_half(both, half)), (sent, of_half(both, 1 - half))):
        for slot, resp in enumerate(responses):
            live = jnp.where(pos < lengths[0, resp], dr[0, resp].astype(F32), 0.0)
            out[0, slot] = stack_heads(qr[0, resp])
            out[1, slot] = stack_heads(live.astype(BF16))
    own[0, 2] = stack_heads(qp[0])
    own[1, 2] = stack_heads(dp[0])
    done[...] = jnp.zeros_like(done)


def block_kernel(lengths, kr, vr, kp, vp, got, _, block):
    half_rows(block, kr, vr, kp, vp, of_half(dealt(lengths), place()[0]))
    block[HALF_ROWS:] = got[...]


def tile_at(kv, part, tile, size=TILE):
    at = pl.ds(tile * TILE_BLOCKS, size // ROWS)
    return [kv[at, part, kind].reshape(size, HD) for kind in range(2)]


def token_factor(total):
    return TOKENS / (2.0 * total[0:1])


def attend(
    tail, z, kv, q_ref, d_ref, part, high, shared, acc, factor,
    dq_out, dq1, kept_s, kept_g,
):
    q, d = q_ref[...], d_ref[...]
    tiles = [(0, 0), (0, 1)] if shared else []
    base = len(tiles)

    def rows_of(place, size):
        return pl.ds(pl.multiple_of(place * TILE, TILE), size)

    def over_tiles(body, now):
        for own, tile in tiles:
            now = body(now, own, tile, tile, TILE, False)
        now = lax.fori_loop(0, high, lambda tile, now: body(now, part, tile, base + tile, TILE, False), now)
        return body(now, part, high, base + high, tail, True)

    def scores(top, part, tile, place, size, masked):
        keys, _ = tile_at(kv, part, tile, size)
        s = dot_nt(keys, q) * (SCALE * LOG2E)
        if masked:
            ahead = lax.broadcasted_iota(jnp.int32, s.shape, 0) - (
                lax.broadcasted_iota(jnp.int32, s.shape, 1) & (ROWS - 1)
            )
            s = jnp.where(ahead <= z * ROWS, s, NEG)
        kept_s[rows_of(place, size)] = s
        return jnp.maximum(top, jnp.max(fold(s), axis=0))

    top = over_tiles(scores, jnp.full((8, CHUNK), NEG, F32))
    top = jnp.max(top, axis=0, keepdims=True)

    def sums(now, part, tile, place, size, masked):
        _, values = tile_at(kv, part, tile, size)
        at = rows_of(place, size)
        g = dot_nt(values, d)
        e = jnp.exp2(kept_s[at] - top)
        kept_s[at] = e
        kept_g[at] = g
        return now[0] + jnp.sum(fold(e), axis=0), now[1] + jnp.sum(fold(e * g), axis=0)

    now = over_tiles(sums, (jnp.zeros((8, CHUNK), F32), jnp.zeros((8, CHUNK), F32)))
    total, mixed = (jnp.sum(value, axis=0, keepdims=True) for value in now)
    inverse = 1.0 / total
    delta = mixed * inverse

    def grads(now, part, tile, place, size, masked):
        keys, _ = tile_at(kv, part, tile, size)
        at = rows_of(place, size)
        w = kept_s[at] * inverse
        grad_s = (w * (kept_g[at] - delta)).astype(BF16)
        dv = dot_nn(w.astype(BF16), d)
        dk = dot_nn(grad_s, q)
        dq1[...] += dot_tn(keys, grad_s)
        at = pl.ds(tile * TILE_BLOCKS, size // ROWS)
        acc[at, part, 0] += dk.reshape(size // ROWS, ROWS, HD)
        acc[at, part, 1] += dv.reshape(size // ROWS, ROWS, HD)
        return now

    dq1[...] = jnp.zeros_like(dq1)
    over_tiles(grads, 0)
    dq_out[...] = (jnp.transpose(dq1[...]) * factor).astype(BF16)


def main_kernel(lengths, total, own, got, *rest):
    blocks, rest = rest[:ZN], rest[ZN:]
    dqp_out, dq_own, dq_pair, rest = rest[0], rest[1], rest[2], rest[3:]
    terms, (far, kv, acc, q_st, d_st, dq_st, *work) = rest[:ZN], rest[ZN:]
    half, z = place()
    factor = token_factor(total) * SCALE
    for step, block in enumerate(blocks):
        for which in range(2):
            at = (half ^ which) * ZN + ((z - step) & (ZN - 1))
            rows = block[which * HALF_ROWS : (which + 1) * HALF_ROWS]
            kv[at] = rows.reshape(3, 2, ROWS, HD)
    acc[...] = jnp.zeros_like(acc)
    dq_st[...] = jnp.zeros_like(dq_st)
    for slot in range(2):
        for kind, ref in enumerate((q_st, d_st)):
            ref[2 * slot] = own[kind, slot]
            ref[2 * slot + 1] = got[kind, slot]
    first, second = of_half(dealt(lengths), half)

    def all_rows(tail):
        attend(
            tail, z, kv, own.at[0, 2], own.at[1, 2], 0, half, False, acc, factor, dqp_out, *work
        )

        def one(chunk, carried):
            slot = chunk >> 1
            high = half ^ (chunk & 1)

            @pl.when((high * ZN + z) * ROWS < lengths[0, jnp.where(slot == 0, first, second)])
            def _():
                attend(
                    tail, z, kv, q_st.at[chunk], d_st.at[chunk], 1 + slot, high, True, acc,
                    factor, dq_st.at[chunk], *work,
                )

            return carried

        lax.fori_loop(0, 4, one, 0)

    pl.when(z < ZN // 2)(lambda: all_rows(TILE // 2))
    pl.when(z >= ZN // 2)(lambda: all_rows(TILE))
    for slot in range(2):
        dq_own[slot] = dq_st[2 * slot]
        dq_pair[slot] = dq_st[2 * slot + 1]
    for step, out in enumerate(terms):
        for which in range(2):
            at = (half ^ which) * ZN + ((z + step) & (ZN - 1))
            rows = acc[at].reshape(HALF_ROWS, HD).astype(BF16)
            if step == ZN // 2:
                (out, far)[which][...] = rows
            else:
                out[which * HALF_ROWS : (which + 1) * HALF_ROWS] = rows


def add_kernel(first, got, term, out):
    rows = slice(first, first + got.shape[0])
    if got.shape != term.shape:
        out[...] = term[...]
    out[rows] = (got[...].astype(F32) + term[rows].astype(F32)).astype(BF16)


def column_kernel(own, up, down, mine, sent):
    total = own[...].astype(F32) + up[...].astype(F32) + down[...].astype(F32)
    mine[...] = total[:HALF_ROWS]
    sent[...] = total[HALF_ROWS:].astype(BF16)


def rows_kernel(lengths, prefix, own, got, prefix_out, out):
    prefix_out[0] = unstack_heads(prefix[...])
    half, _ = place()
    both = dealt(lengths)
    for slot, resp in enumerate(of_half(both, half)):
        out[0, resp] = unstack_heads(own[slot])
    for slot, resp in enumerate(of_half(both, 1 - half)):
        out[0, resp] = unstack_heads(got[slot])


def sums_kernel(lengths, total, mine, got, dkp, dvp, dkr, dvr):
    half, _ = place()
    both = dealt(lengths)
    factor = token_factor(total)
    for kind, outs, by in ((0, (dkp, dkr), factor * SCALE), (1, (dvp, dvr), factor)):
        outs[0][0] = (mine[kind * ROWS : (kind + 1) * ROWS] + got[kind * ROWS : (kind + 1) * ROWS].astype(F32)) * by
        for source, responses in ((mine, of_half(both, half)), (got, of_half(both, 1 - half))):
            for slot, resp in enumerate(responses):
                at = ((1 + slot) * 2 + kind) * ROWS
                outs[1][0, resp] = source[at : at + ROWS].astype(F32) * by


def shape(dims, dtype):
    return jax.ShapeDtypeStruct(dims, dtype)


def call(kernel, kinds, outs, scratch=(), flops=1 << 20, name=None, vmem=8):
    spec = {"s": SMEM, "v": VMEM}
    return pl.pallas_call(
        kernel,
        out_shape=outs,
        in_specs=[spec[kind] for kind in kinds],
        out_specs=[VMEM] * len(outs),
        scratch_shapes=list(scratch),
        name=name,
        cost_estimate=pl.CostEstimate(flops=flops, bytes_accessed=2 << 20, transcendentals=0),
        compiler_params=pltpu.CompilerParams(vmem_limit_bytes=vmem << 20),
    )


def per_device(
    q_prefix, q_resp, k_prefix, v_prefix, k_resp, v_resp, dout_prefix, dout_resp, lengths
):
    pair = [(i, (i + ZN) % (2 * ZN)) for i in range(2 * ZN)]

    def swap(value):
        return lax.ppermute(value, "resp", pair)

    def shift(value, by):
        moves = [(c + i, c + (i + by) % ZN) for c in (0, ZN) for i in range(ZN)]
        return lax.ppermute(value, "resp", moves)

    def add_count(value, step):
        return lax.ppermute(value, "prompt", [(i, i ^ step) for i in range(PROMPTS)])

    count = shape((8, HD), F32)
    half_keys = shape((HALF_ROWS, HD), BF16)
    sent, total = call(
        keys_kernel, "svvvv", [half_keys, count], name="keys", vmem=60
    )(lengths, k_resp, v_resp, k_prefix, v_prefix)
    kv_got = swap(sent)
    own, q_sent, built = call(
        queries_kernel, "svvvv",
        [shape((2, 3, CHUNK, HD), BF16), shape((2, 2, CHUNK, HD), BF16), count],
        name="queries", vmem=24,
    )(lengths, q_resp, dout_resp, q_prefix, dout_prefix)
    got = swap(q_sent)
    (block,) = call(
        block_kernel, "svvvvvv", [shape((2 * HALF_ROWS, HD), BF16)], name="block"
    )(lengths, k_resp, v_resp, k_prefix, v_prefix, kv_got, built)
    blocks = [block] * ZN
    for step in range(1, ZN // 2 + 1):
        before = blocks[step - 1]
        if step > 1:
            total = total + add_count(total, (2, 1, 4)[step - 2])
            before, total = lax.optimization_barrier((before, total))
        blocks[step] = shift(before, 1)
        if step < ZN // 2:
            blocks[ZN - step] = shift(blocks[(ZN - step + 1) % ZN], -1)
    total = total + add_count(total, 8)
    rows = shape((2, CHUNK, HD), BF16)
    whole_keys = shape((2 * HALF_ROWS, HD), BF16)
    dqp, dq_own, dq_pair, *terms, down = call(
        main_kernel, "s" + "v" * (ZN + 3),
        [shape((CHUNK, HD), BF16), rows, rows]
        + [whole_keys] * (ZN // 2) + [half_keys] + [whole_keys] * (ZN // 2 - 1) + [half_keys],
        [pltpu.VMEM((2 * ZN, 3, 2, ROWS, HD), BF16), pltpu.VMEM((2 * ZN, 3, 2, ROWS, HD), F32),
         pltpu.VMEM((4, CHUNK, HD), BF16), pltpu.VMEM((4, CHUNK, HD), BF16),
         pltpu.VMEM((4, CHUNK, HD), BF16), pltpu.VMEM((HD, CHUNK), F32),
         pltpu.VMEM((4 * TILE, CHUNK), F32), pltpu.VMEM((4 * TILE, CHUNK), F32)],
        9 << 30, "main", BIG,
    )(lengths, total, own, got, *blocks)

    def add(got, term, first=0):
        body = functools.partial(add_kernel, first)
        return call(body, "vv", [whole_keys], name="add")(got, term)[0]

    up = terms[ZN // 2]
    for step in range(ZN // 2 - 1, 0, -1):
        up = add(shift(up, 1), terms[step])
        down = add(shift(down, -1), terms[ZN - step], HALF_ROWS if step == ZN // 2 - 1 else 0)
    mine, sent = call(column_kernel, "vvv", [shape((HALF_ROWS, HD), F32), half_keys], name="column")(
        terms[0], shift(up, 1), shift(down, -1)
    )
    terms_got = swap(sent)
    dq_got = swap(dq_pair)
    dqp_out, dq_all = call(
        rows_kernel, "svvv",
        [shape((1, ROWS, HEADS * HD), BF16), shape((1, RESPS, ROWS, HEADS * HD), BF16)],
        name="rows",
    )(lengths, dqp, dq_own, dq_got)
    prefix_out = shape((1, ROWS, HD), F32)
    resp_out = shape((1, RESPS, ROWS, HD), F32)
    dkp, dvp, dkr, dvr = call(
        sums_kernel, "svvv", [prefix_out, prefix_out, resp_out, resp_out],
        name="sums",
    )(lengths, total, mine, terms_got)
    return dqp_out, dq_all, dkp, dvp, dkr, dvr


def solution(mesh):
    rows = P("prompt", "resp", None)
    resp_rows = P("prompt", None, "resp", None)
    return jax.shard_map(
        per_device,
        mesh=mesh,
        in_specs=(
            rows, resp_rows, rows, rows, resp_rows, resp_rows, rows, resp_rows, P("prompt", None),
        ),
        out_specs=(rows, resp_rows, rows, rows, resp_rows, resp_rows),
        check_vma=False,
    )
```

```python
import functools

import jax
import jax.numpy as jnp
from jax import lax
from jax.experimental import pallas as pl
from jax.experimental.pallas import tpu as pltpu
from jax.sharding import PartitionSpec as P

HD = 128
HEADS = 8
ROWS = 64
CHUNK = ROWS * HEADS
ZN = 8
PROMPTS = 16
RESPS = 4
TOKENS = 65536.0
NEG = -1e30
SCALE = HD**-0.5
LOG2E = 1.4426950408889634
TILE_BLOCKS = 8
TILE = TILE_BLOCKS * ROWS
BIG = 30
HALF_ROWS = 6 * ROWS
VMEM = pl.BlockSpec(memory_space=pltpu.VMEM)
SMEM = pl.BlockSpec(memory_space=pltpu.SMEM)
F32 = jnp.float32
BF16 = jnp.bfloat16


def dot_nt(a, b):
    return lax.dot_general(a, b, (((1,), (1,)), ((), ())), preferred_element_type=F32)


def dot_tn(a, b):
    return lax.dot_general(a, b, (((0,), (0,)), ((), ())), preferred_element_type=F32)


def dot_nn(a, b):
    return lax.dot_general(a, b, (((1,), (0,)), ((), ())), preferred_element_type=F32)


def stack_heads(rows):
    return jnp.concatenate([rows[:, h * HD : (h + 1) * HD] for h in range(HEADS)], axis=0)


def unstack_heads(rows):
    return jnp.concatenate([rows[h * ROWS : (h + 1) * ROWS] for h in range(HEADS)], axis=1)


def place():
    me = lax.axis_index("resp")
    return me >> 3, me & (ZN - 1)


def dealt(lengths):
    size = [lengths[0, i] for i in range(RESPS)]
    rank = []
    for i in range(RESPS):
        before = [
            ((size[j] >= size[i]) if j < i else (size[j] > size[i])).astype(jnp.int32)
            for j in range(RESPS)
            if j != i
        ]
        rank.append(before[0] + before[1] + before[2])
    at = [
        sum(jnp.where(rank[i] == k, i, 0) for i in range(1, RESPS)) for k in range(RESPS)
    ]
    return (at[1], at[2]), (at[0], at[3])


def of_half(both, half):
    return tuple(jnp.where(half == 0, a, b) for a, b in zip(*both))


def fold(value):
    return value.reshape(value.shape[0] // 8, 8, CHUNK)


def half_rows(out, kr, vr, kp, vp, responses):
    rows = [kp[0], vp[0]]
    for resp in responses:
        rows += [kr[0, resp], vr[0, resp]]
    for at, value in enumerate(rows):
        out[at * ROWS : (at + 1) * ROWS] = value


def keys_kernel(lengths, kr, vr, kp, vp, sent, count):
    half, _ = place()
    half_rows(sent, kr, vr, kp, vp, of_half(dealt(lengths), 1 - half))
    total = lengths[0, 0] + lengths[0, 1] + lengths[0, 2] + lengths[0, 3]
    count[...] = jnp.full(count.shape, total, jnp.int32).astype(F32)


def queries_kernel(lengths, qr, dr, qp, dp, own, sent, done):
    half, z = place()
    both = dealt(lengths)
    pos = (half * ZN + z) * ROWS + lax.broadcasted_iota(jnp.int32, (ROWS, HEADS * HD), 0)
    for out, responses in ((own, of_half(both, half)), (sent, of_half(both, 1 - half))):
        for slot, resp in enumerate(responses):
            live = jnp.where(pos < lengths[0, resp], dr[0, resp].astype(F32), 0.0)
            out[0, slot] = stack_heads(qr[0, resp])
            out[1, slot] = stack_heads(live.astype(BF16))
    own[0, 2] = stack_heads(qp[0])
    own[1, 2] = stack_heads(dp[0])
    done[...] = jnp.zeros_like(done)


def block_kernel(lengths, kr, vr, kp, vp, got, _, block):
    half_rows(block, kr, vr, kp, vp, of_half(dealt(lengths), place()[0]))
    block[HALF_ROWS:] = got[...]


def tile_at(kv, part, tile, size=TILE):
    at = pl.ds(tile * TILE_BLOCKS, size // ROWS)
    return [kv[at, part, kind].reshape(size, HD) for kind in range(2)]


def token_factor(total):
    return TOKENS / (2.0 * total[0:1])


def attend(
    tail, z, kv, q_ref, d_ref, part, high, shared, acc, factor,
    dq_out, dq1, kept_s, kept_g,
):
    q, d = q_ref[...], d_ref[...]
    tiles = [(0, 0), (0, 1)] if shared else []
    base = len(tiles)

    def rows_of(place, size):
        return pl.ds(pl.multiple_of(place * TILE, TILE), size)

    def over_tiles(body, now):
        for own, tile in tiles:
            now = body(now, own, tile, tile, TILE, False)
        now = lax.fori_loop(0, high, lambda tile, now: body(now, part, tile, base + tile, TILE, False), now)
        return body(now, part, high, base + high, tail, True)

    def scores(top, part, tile, place, size, masked):
        keys, _ = tile_at(kv, part, tile, size)
        s = dot_nt(keys, q) * (SCALE * LOG2E)
        if masked:
            ahead = lax.broadcasted_iota(jnp.int32, s.shape, 0) - (
                lax.broadcasted_iota(jnp.int32, s.shape, 1) & (ROWS - 1)
            )
            s = jnp.where(ahead <= z * ROWS, s, NEG)
        kept_s[rows_of(place, size)] = s
        return jnp.maximum(top, jnp.max(fold(s), axis=0))

    top = over_tiles(scores, jnp.full((8, CHUNK), NEG, F32))
    top = jnp.max(top, axis=0, keepdims=True)

    def sums(now, part, tile, place, size, masked):
        _, values = tile_at(kv, part, tile, size)
        at = rows_of(place, size)
        g = dot_nt(values, d)
        e = jnp.exp2(kept_s[at] - top)
        kept_s[at] = e
        kept_g[at] = g
        return now[0] + jnp.sum(fold(e), axis=0), now[1] + jnp.sum(fold(e * g), axis=0)

    now = over_tiles(sums, (jnp.zeros((8, CHUNK), F32), jnp.zeros((8, CHUNK), F32)))
    total, mixed = (jnp.sum(value, axis=0, keepdims=True) for value in now)
    inverse = 1.0 / total
    delta = mixed * inverse

    def grads(now, part, tile, place, size, masked):
        keys, _ = tile_at(kv, part, tile, size)
        at = rows_of(place, size)
        w = kept_s[at] * inverse
        grad_s = (w * (kept_g[at] - delta)).astype(BF16)
        dv = dot_nn(w.astype(BF16), d)
        dk = dot_nn(grad_s, q)
        dq1[...] += dot_tn(keys, grad_s)
        at = pl.ds(tile * TILE_BLOCKS, size // ROWS)
        acc[at, part, 0] += dk.reshape(size // ROWS, ROWS, HD)
        acc[at, part, 1] += dv.reshape(size // ROWS, ROWS, HD)
        return now

    dq1[...] = jnp.zeros_like(dq1)
    over_tiles(grads, 0)
    dq_out[...] = (jnp.transpose(dq1[...]) * factor).astype(BF16)


def main_kernel(lengths, total, own, got, *rest):
    blocks, rest = rest[:ZN], rest[ZN:]
    dqp_out, dq_own, dq_pair, rest = rest[0], rest[1], rest[2], rest[3:]
    terms, (far, near, kv, acc, q_st, d_st, dq_st, *work) = rest[:ZN], rest[ZN:]
    half, z = place()
    factor = token_factor(total) * SCALE
    for step, block in enumerate(blocks):
        for which in range(2):
            at = (half ^ which) * ZN + ((z - step) & (ZN - 1))
            rows = block[which * HALF_ROWS : (which + 1) * HALF_ROWS]
            kv[at] = rows.reshape(3, 2, ROWS, HD)
    acc[...] = jnp.zeros_like(acc)
    dq_st[...] = jnp.zeros_like(dq_st)
    for slot in range(2):
        for kind, ref in enumerate((q_st, d_st)):
            ref[2 * slot] = own[kind, slot]
            ref[2 * slot + 1] = got[kind, slot]
    first, second = of_half(dealt(lengths), half)

    def all_rows(tail):
        attend(
            tail, z, kv, own.at[0, 2], own.at[1, 2], 0, half, False, acc, factor, dqp_out, *work
        )

        def one(chunk, carried):
            slot = chunk >> 1
            high = half ^ (chunk & 1)

            @pl.when((high * ZN + z) * ROWS < lengths[0, jnp.where(slot == 0, first, second)])
            def _():
                attend(
                    tail, z, kv, q_st.at[chunk], d_st.at[chunk], 1 + slot, high, True, acc,
                    factor, dq_st.at[chunk], *work,
                )

            return carried

        lax.fori_loop(0, 4, one, 0)

    pl.when(z < ZN // 2)(lambda: all_rows(TILE // 2))
    pl.when(z >= ZN // 2)(lambda: all_rows(TILE))
    for slot in range(2):
        dq_own[slot] = dq_st[2 * slot]
        dq_pair[slot] = dq_st[2 * slot + 1]
    for step, out in enumerate(terms):
        for which in range(2):
            at = (half ^ which) * ZN + ((z + step) & (ZN - 1))
            rows = acc[at].reshape(HALF_ROWS, HD).astype(BF16)
            if step == 0:
                (out, near)[which][...] = rows
            elif step == ZN // 2:
                (out, far)[which][...] = rows
            else:
                out[which * HALF_ROWS : (which + 1) * HALF_ROWS] = rows


def add_kernel(first, got, term, out):
    rows = slice(first, first + got.shape[0])
    if got.shape != term.shape:
        out[...] = term[...]
    out[rows] = (got[...].astype(F32) + term[rows].astype(F32)).astype(BF16)


def last_add_kernel(got, term, same, other):
    for at, out in enumerate((same, other)):
        rows = slice(at * HALF_ROWS, (at + 1) * HALF_ROWS)
        out[...] = (got[rows].astype(F32) + term[rows].astype(F32)).astype(BF16)


def rows_kernel(lengths, prefix, own, got, prefix_out, out):
    prefix_out[0] = unstack_heads(prefix[...])
    half, _ = place()
    both = dealt(lengths)
    for slot, resp in enumerate(of_half(both, half)):
        out[0, resp] = unstack_heads(own[slot])
    for slot, resp in enumerate(of_half(both, 1 - half)):
        out[0, resp] = unstack_heads(got[slot])


def sums_kernel(lengths, total, *rest):
    mine, got, (dkp, dvp, dkr, dvr) = rest[:3], rest[3:6], rest[6:]
    half, _ = place()
    both = dealt(lengths)
    factor = token_factor(total)

    def summed(sources, block):
        rows = slice(block * ROWS, (block + 1) * ROWS)
        return sum(source[rows].astype(F32) for source in sources)

    for kind, outs, by in ((0, (dkp, dkr), factor * SCALE), (1, (dvp, dvr), factor)):
        outs[0][0] = (summed(mine, kind) + summed(got, kind)) * by
        for sources, responses in ((mine, of_half(both, half)), (got, of_half(both, 1 - half))):
            for slot, resp in enumerate(responses):
                outs[1][0, resp] = summed(sources, (1 + slot) * 2 + kind) * by


def shape(dims, dtype):
    return jax.ShapeDtypeStruct(dims, dtype)


def call(kernel, kinds, outs, scratch=(), flops=1 << 20, name=None, vmem=8):
    spec = {"s": SMEM, "v": VMEM}
    return pl.pallas_call(
        kernel,
        out_shape=outs,
        in_specs=[spec[kind] for kind in kinds],
        out_specs=[VMEM] * len(outs),
        scratch_shapes=list(scratch),
        name=name,
        cost_estimate=pl.CostEstimate(flops=flops, bytes_accessed=2 << 20, transcendentals=0),
        compiler_params=pltpu.CompilerParams(vmem_limit_bytes=vmem << 20),
    )


def per_device(
    q_prefix, q_resp, k_prefix, v_prefix, k_resp, v_resp, dout_prefix, dout_resp, lengths
):
    pair = [(i, (i + ZN) % (2 * ZN)) for i in range(2 * ZN)]

    def swap(value):
        return lax.ppermute(value, "resp", pair)

    def shift(value, by):
        moves = [(c + i, c + (i + by) % ZN) for c in (0, ZN) for i in range(ZN)]
        return lax.ppermute(value, "resp", moves)

    def add_count(value, step):
        return lax.ppermute(value, "prompt", [(i, i ^ step) for i in range(PROMPTS)])

    count = shape((8, HD), F32)
    half_keys = shape((HALF_ROWS, HD), BF16)
    sent, total = call(
        keys_kernel, "svvvv", [half_keys, count], name="keys", vmem=60
    )(lengths, k_resp, v_resp, k_prefix, v_prefix)
    kv_got = swap(sent)
    own, q_sent, built = call(
        queries_kernel, "svvvv",
        [shape((2, 3, CHUNK, HD), BF16), shape((2, 2, CHUNK, HD), BF16), count],
        name="queries", vmem=24,
    )(lengths, q_resp, dout_resp, q_prefix, dout_prefix)
    got = swap(q_sent)
    (block,) = call(
        block_kernel, "svvvvvv", [shape((2 * HALF_ROWS, HD), BF16)], name="block"
    )(lengths, k_resp, v_resp, k_prefix, v_prefix, kv_got, built)
    blocks = [block] * ZN
    for step in range(1, ZN // 2 + 1):
        before = blocks[step - 1]
        if step > 1:
            total = total + add_count(total, (2, 1, 4)[step - 2])
            before, total = lax.optimization_barrier((before, total))
        blocks[step] = shift(before, 1)
        if step < ZN // 2:
            blocks[ZN - step] = shift(blocks[(ZN - step + 1) % ZN], -1)
    total = total + add_count(total, 8)
    rows = shape((2, CHUNK, HD), BF16)
    whole_keys = shape((2 * HALF_ROWS, HD), BF16)
    dqp, dq_own, dq_pair, *terms, down, near = call(
        main_kernel, "s" + "v" * (ZN + 3),
        [shape((CHUNK, HD), BF16), rows, rows]
        + ([half_keys] + [whole_keys] * (ZN // 2 - 1)) * 2 + [half_keys] * 2,
        [pltpu.VMEM((2 * ZN, 3, 2, ROWS, HD), BF16), pltpu.VMEM((2 * ZN, 3, 2, ROWS, HD), F32),
         pltpu.VMEM((4, CHUNK, HD), BF16), pltpu.VMEM((4, CHUNK, HD), BF16),
         pltpu.VMEM((4, CHUNK, HD), BF16), pltpu.VMEM((HD, CHUNK), F32),
         pltpu.VMEM((4 * TILE, CHUNK), F32), pltpu.VMEM((4 * TILE, CHUNK), F32)],
        9 << 30, "main", BIG,
    )(lengths, total, own, got, *blocks)

    def add(got, term, first=0):
        body = functools.partial(add_kernel, first)
        return call(body, "vv", [whole_keys], name="add")(got, term)[0]

    def last(got, term, by):
        same, other = call(last_add_kernel, "vv", [half_keys] * 2, name="last")(got, term)
        moves = [
            (c + i, (c + ZN) % (2 * ZN) + (i + by) % ZN) for c in (0, ZN) for i in range(ZN)
        ]
        return shift(same, by), lax.ppermute(other, "resp", moves)

    up = terms[ZN // 2]
    for step in range(ZN // 2 - 1, 1, -1):
        up = add(shift(up, 1), terms[step])
        down = add(shift(down, -1), terms[ZN - step], HALF_ROWS if step == ZN // 2 - 1 else 0)
    up, up_got = last(shift(up, 1), terms[1], 1)
    down, down_got = last(shift(down, -1), terms[ZN - 1], -1)
    near_got = swap(near)
    dq_got = swap(dq_pair)
    dqp_out, dq_all = call(
        rows_kernel, "svvv",
        [shape((1, ROWS, HEADS * HD), BF16), shape((1, RESPS, ROWS, HEADS * HD), BF16)],
        name="rows",
    )(lengths, dqp, dq_own, dq_got)
    prefix_out = shape((1, ROWS, HD), F32)
    resp_out = shape((1, RESPS, ROWS, HD), F32)
    dkp, dvp, dkr, dvr = call(
        sums_kernel, "s" + "v" * 7, [prefix_out, prefix_out, resp_out, resp_out],
        name="sums",
    )(lengths, total, terms[0], up, down, near_got, up_got, down_got)
    return dqp_out, dq_all, dkp, dvp, dkr, dvr


def solution(mesh):
    rows = P("prompt", "resp", None)
    resp_rows = P("prompt", None, "resp", None)
    return jax.shard_map(
        per_device,
        mesh=mesh,
        in_specs=(
            rows, resp_rows, rows, rows, resp_rows, resp_rows, rows, resp_rows, P("prompt", None),
        ),
        out_specs=(rows, resp_rows, rows, rows, resp_rows, resp_rows),
        check_vma=False,
    )
```

```python
import functools

import jax
import jax.numpy as jnp
from jax import lax
from jax.experimental import pallas as pl
from jax.experimental.pallas import tpu as pltpu
from jax.sharding import PartitionSpec as P

HD = 128
HEADS = 8
ROWS = 64
CHUNK = ROWS * HEADS
ZN = 8
PROMPTS = 16
RESPS = 4
TOKENS = 65536.0
NEG = -1e30
SCALE = HD**-0.5
LOG2E = 1.4426950408889634
TILE_BLOCKS = 8
TILE = TILE_BLOCKS * ROWS
BIG = 30
HALF_ROWS = 6 * ROWS
VMEM = pl.BlockSpec(memory_space=pltpu.VMEM)
SMEM = pl.BlockSpec(memory_space=pltpu.SMEM)
F32 = jnp.float32
BF16 = jnp.bfloat16


def dot_nt(a, b):
    return lax.dot_general(a, b, (((1,), (1,)), ((), ())), preferred_element_type=F32)


def dot_tn(a, b):
    return lax.dot_general(a, b, (((0,), (0,)), ((), ())), preferred_element_type=F32)


def dot_nn(a, b):
    return lax.dot_general(a, b, (((1,), (0,)), ((), ())), preferred_element_type=F32)


def stack_heads(rows):
    return jnp.concatenate([rows[:, h * HD : (h + 1) * HD] for h in range(HEADS)], axis=0)


def unstack_heads(rows):
    return jnp.concatenate([rows[h * ROWS : (h + 1) * ROWS] for h in range(HEADS)], axis=1)


def place():
    me = lax.axis_index("resp")
    return me >> 3, me & (ZN - 1)


def dealt(lengths):
    size = [lengths[0, i] for i in range(RESPS)]
    rank = []
    for i in range(RESPS):
        before = [
            ((size[j] >= size[i]) if j < i else (size[j] > size[i])).astype(jnp.int32)
            for j in range(RESPS)
            if j != i
        ]
        rank.append(before[0] + before[1] + before[2])
    at = [
        sum(jnp.where(rank[i] == k, i, 0) for i in range(1, RESPS)) for k in range(RESPS)
    ]
    return (at[1], at[2]), (at[0], at[3])


def of_half(both, half):
    return tuple(jnp.where(half == 0, a, b) for a, b in zip(*both))


def fold(value):
    return value.reshape(value.shape[0] // 8, 8, CHUNK)


def half_rows(out, kr, vr, kp, vp, responses):
    rows = [kp[0], vp[0]]
    for resp in responses:
        rows += [kr[0, resp], vr[0, resp]]
    for at, value in enumerate(rows):
        out[at * ROWS : (at + 1) * ROWS] = value


def keys_kernel(lengths, kr, vr, kp, vp, sent, count):
    half, _ = place()
    half_rows(sent, kr, vr, kp, vp, of_half(dealt(lengths), 1 - half))
    total = lengths[0, 0] + lengths[0, 1] + lengths[0, 2] + lengths[0, 3]
    count[...] = jnp.full(count.shape, total, jnp.int32).astype(F32)


def queries_kernel(lengths, qr, dr, qp, dp, own, sent, done):
    half, z = place()
    both = dealt(lengths)
    pos = (half * ZN + z) * ROWS + lax.broadcasted_iota(jnp.int32, (ROWS, HEADS * HD), 0)
    for out, responses in ((own, of_half(both, half)), (sent, of_half(both, 1 - half))):
        for slot, resp in enumerate(responses):
            live = jnp.where(pos < lengths[0, resp], dr[0, resp].astype(F32), 0.0)
            out[0, slot] = stack_heads(qr[0, resp])
            out[1, slot] = stack_heads(live.astype(BF16))
    own[0, 2] = stack_heads(qp[0])
    own[1, 2] = stack_heads(dp[0])
    done[...] = jnp.zeros_like(done)


def block_kernel(lengths, kr, vr, kp, vp, got, _, block):
    half_rows(block, kr, vr, kp, vp, of_half(dealt(lengths), place()[0]))
    block[HALF_ROWS:] = got[...]


def tile_at(kv, part, tile, size=TILE):
    at = pl.ds(tile * TILE_BLOCKS, size // ROWS)
    return [kv[at, part, kind].reshape(size, HD) for kind in range(2)]


def token_factor(total):
    return TOKENS / (2.0 * total[0:1])


def attend(
    tail, z, kv, q_ref, d_ref, part, high, shared, acc, factor,
    dq_out, dq1, kept_s, kept_g,
):
    q, d = q_ref[...], d_ref[...]
    tiles = [(0, 0), (0, 1)] if shared else []
    base = len(tiles)

    def rows_of(place, size):
        return pl.ds(pl.multiple_of(place * TILE, TILE), size)

    def over_tiles(body, now):
        for own, tile in tiles:
            now = body(now, own, tile, tile, TILE, False)
        now = lax.fori_loop(0, high, lambda tile, now: body(now, part, tile, base + tile, TILE, False), now)
        return body(now, part, high, base + high, tail, True)

    def scores(top, part, tile, place, size, masked):
        keys, _ = tile_at(kv, part, tile, size)
        s = dot_nt(keys, q) * (SCALE * LOG2E)
        if masked:
            ahead = lax.broadcasted_iota(jnp.int32, s.shape, 0) - (
                lax.broadcasted_iota(jnp.int32, s.shape, 1) & (ROWS - 1)
            )
            s = jnp.where(ahead <= z * ROWS, s, NEG)
        kept_s[rows_of(place, size)] = s
        return jnp.maximum(top, jnp.max(fold(s), axis=0))

    top = over_tiles(scores, jnp.full((8, CHUNK), NEG, F32))
    top = jnp.max(top, axis=0, keepdims=True)

    def sums(now, part, tile, place, size, masked):
        _, values = tile_at(kv, part, tile, size)
        at = rows_of(place, size)
        g = dot_nt(values, d)
        e = jnp.exp2(kept_s[at] - top)
        kept_s[at] = e
        kept_g[at] = g
        return now[0] + jnp.sum(fold(e), axis=0), now[1] + jnp.sum(fold(e * g), axis=0)

    now = over_tiles(sums, (jnp.zeros((8, CHUNK), F32), jnp.zeros((8, CHUNK), F32)))
    total, mixed = (jnp.sum(value, axis=0, keepdims=True) for value in now)
    inverse = 1.0 / total
    delta = mixed * inverse

    def grads(now, part, tile, place, size, masked):
        keys, _ = tile_at(kv, part, tile, size)
        at = rows_of(place, size)
        w = kept_s[at] * inverse
        grad_s = (w * (kept_g[at] - delta)).astype(BF16)
        dv = dot_nn(w.astype(BF16), d)
        dk = dot_nn(grad_s, q)
        dq1[...] += dot_tn(keys, grad_s)
        at = pl.ds(tile * TILE_BLOCKS, size // ROWS)
        acc[at, part, 0] += dk.reshape(size // ROWS, ROWS, HD)
        acc[at, part, 1] += dv.reshape(size // ROWS, ROWS, HD)
        return now

    dq1[...] = jnp.zeros_like(dq1)
    over_tiles(grads, 0)
    dq_out[...] = (jnp.transpose(dq1[...]) * factor).astype(BF16)


def main_kernel(lengths, total, own, got, *rest):
    blocks, rest = rest[:ZN], rest[ZN:]
    dqp_out, dq_own, dq_pair, rest = rest[0], rest[1], rest[2], rest[3:]
    terms, (far, near, kv, acc, q_st, d_st, dq_st, *work) = rest[:ZN], rest[ZN:]
    half, z = place()
    factor = token_factor(total) * SCALE
    for step, block in enumerate(blocks):
        for which in range(2):
            at = (half ^ which) * ZN + ((z - step) & (ZN - 1))
            rows = block[which * HALF_ROWS : (which + 1) * HALF_ROWS]
            kv[at] = rows.reshape(3, 2, ROWS, HD)
    acc[...] = jnp.zeros_like(acc)
    dq_st[...] = jnp.zeros_like(dq_st)
    for slot in range(2):
        for kind, ref in enumerate((q_st, d_st)):
            ref[2 * slot] = own[kind, slot]
            ref[2 * slot + 1] = got[kind, slot]
    first, second = of_half(dealt(lengths), half)

    def all_rows(tail):
        attend(
            tail, z, kv, own.at[0, 2], own.at[1, 2], 0, half, False, acc, factor, dqp_out, *work
        )

        def one(chunk, carried):
            slot = chunk >> 1
            high = half ^ (chunk & 1)

            @pl.when((high * ZN + z) * ROWS < lengths[0, jnp.where(slot == 0, first, second)])
            def _():
                attend(
                    tail, z, kv, q_st.at[chunk], d_st.at[chunk], 1 + slot, high, True, acc,
                    factor, dq_st.at[chunk], *work,
                )

            return carried

        lax.fori_loop(0, 4, one, 0)

    pl.when(z < 4)(lambda: all_rows(4 * ROWS))
    pl.when((z == 4) | (z == 5))(lambda: all_rows(6 * ROWS))
    pl.when(z == 6)(lambda: all_rows(7 * ROWS))
    pl.when(z == 7)(lambda: all_rows(TILE))
    for slot in range(2):
        dq_own[slot] = dq_st[2 * slot]
        dq_pair[slot] = dq_st[2 * slot + 1]
    for step, out in enumerate(terms):
        for which in range(2):
            at = (half ^ which) * ZN + ((z + step) & (ZN - 1))
            rows = acc[at].reshape(HALF_ROWS, HD).astype(BF16)
            if step == 0:
                (out, near)[which][...] = rows
            elif step == ZN // 2:
                (out, far)[which][...] = rows
            else:
                out[which * HALF_ROWS : (which + 1) * HALF_ROWS] = rows


def add_kernel(first, got, term, out):
    rows = slice(first, first + got.shape[0])
    if got.shape != term.shape:
        out[...] = term[...]
    out[rows] = (got[...].astype(F32) + term[rows].astype(F32)).astype(BF16)


def last_add_kernel(got, term, same, other):
    for at, out in enumerate((same, other)):
        rows = slice(at * HALF_ROWS, (at + 1) * HALF_ROWS)
        out[...] = (got[rows].astype(F32) + term[rows].astype(F32)).astype(BF16)


def rows_kernel(lengths, prefix, own, got, prefix_out, out):
    prefix_out[0] = unstack_heads(prefix[...])
    half, _ = place()
    both = dealt(lengths)
    for slot, resp in enumerate(of_half(both, half)):
        out[0, resp] = unstack_heads(own[slot])
    for slot, resp in enumerate(of_half(both, 1 - half)):
        out[0, resp] = unstack_heads(got[slot])


def sums_kernel(lengths, total, *rest):
    mine, got, (dkp, dvp, dkr, dvr) = rest[:3], rest[3:6], rest[6:]
    half, _ = place()
    both = dealt(lengths)
    factor = token_factor(total)

    def summed(sources, block):
        rows = slice(block * ROWS, (block + 1) * ROWS)
        return sum(source[rows].astype(F32) for source in sources)

    for kind, outs, by in ((0, (dkp, dkr), factor * SCALE), (1, (dvp, dvr), factor)):
        outs[0][0] = (summed(mine, kind) + summed(got, kind)) * by
        for sources, responses in ((mine, of_half(both, half)), (got, of_half(both, 1 - half))):
            for slot, resp in enumerate(responses):
                outs[1][0, resp] = summed(sources, (1 + slot) * 2 + kind) * by


def shape(dims, dtype):
    return jax.ShapeDtypeStruct(dims, dtype)


def call(kernel, kinds, outs, scratch=(), flops=1 << 20, name=None, vmem=8):
    spec = {"s": SMEM, "v": VMEM}
    return pl.pallas_call(
        kernel,
        out_shape=outs,
        in_specs=[spec[kind] for kind in kinds],
        out_specs=[VMEM] * len(outs),
        scratch_shapes=list(scratch),
        name=name,
        cost_estimate=pl.CostEstimate(flops=flops, bytes_accessed=2 << 20, transcendentals=0),
        compiler_params=pltpu.CompilerParams(vmem_limit_bytes=vmem << 20),
    )


def per_device(
    q_prefix, q_resp, k_prefix, v_prefix, k_resp, v_resp, dout_prefix, dout_resp, lengths
):
    pair = [(i, (i + ZN) % (2 * ZN)) for i in range(2 * ZN)]

    def swap(value):
        return lax.ppermute(value, "resp", pair)

    def shift(value, by):
        moves = [(c + i, c + (i + by) % ZN) for c in (0, ZN) for i in range(ZN)]
        return lax.ppermute(value, "resp", moves)

    def add_count(value, step):
        return lax.ppermute(value, "prompt", [(i, i ^ step) for i in range(PROMPTS)])

    count = shape((8, HD), F32)
    half_keys = shape((HALF_ROWS, HD), BF16)
    sent, total = call(
        keys_kernel, "svvvv", [half_keys, count], name="keys", vmem=60
    )(lengths, k_resp, v_resp, k_prefix, v_prefix)
    kv_got = swap(sent)
    own, q_sent, built = call(
        queries_kernel, "svvvv",
        [shape((2, 3, CHUNK, HD), BF16), shape((2, 2, CHUNK, HD), BF16), count],
        name="queries", vmem=24,
    )(lengths, q_resp, dout_resp, q_prefix, dout_prefix)
    got = swap(q_sent)
    (block,) = call(
        block_kernel, "svvvvvv", [shape((2 * HALF_ROWS, HD), BF16)], name="block"
    )(lengths, k_resp, v_resp, k_prefix, v_prefix, kv_got, built)
    blocks = [block] * ZN
    for step in range(1, ZN // 2 + 1):
        before = blocks[step - 1]
        if step > 1:
            total = total + add_count(total, (2, 1, 4)[step - 2])
            before, total = lax.optimization_barrier((before, total))
        blocks[step] = shift(before, 1)
        if step < ZN // 2:
            blocks[ZN - step] = shift(blocks[(ZN - step + 1) % ZN], -1)
    total = total + add_count(total, 8)
    rows = shape((2, CHUNK, HD), BF16)
    whole_keys = shape((2 * HALF_ROWS, HD), BF16)
    dqp, dq_own, dq_pair, *terms, down, near = call(
        main_kernel, "s" + "v" * (ZN + 3),
        [shape((CHUNK, HD), BF16), rows, rows]
        + ([half_keys] + [whole_keys] * (ZN // 2 - 1)) * 2 + [half_keys] * 2,
        [pltpu.VMEM((2 * ZN, 3, 2, ROWS, HD), BF16), pltpu.VMEM((2 * ZN, 3, 2, ROWS, HD), F32),
         pltpu.VMEM((4, CHUNK, HD), BF16), pltpu.VMEM((4, CHUNK, HD), BF16),
         pltpu.VMEM((4, CHUNK, HD), BF16), pltpu.VMEM((HD, CHUNK), F32),
         pltpu.VMEM((4 * TILE, CHUNK), F32), pltpu.VMEM((4 * TILE, CHUNK), F32)],
        9 << 30, "main", BIG,
    )(lengths, total, own, got, *blocks)

    def add(got, term, first=0):
        body = functools.partial(add_kernel, first)
        return call(body, "vv", [whole_keys], name="add")(got, term)[0]

    def last(got, term, by):
        same, other = call(last_add_kernel, "vv", [half_keys] * 2, name="last")(got, term)
        moves = [
            (c + i, (c + ZN) % (2 * ZN) + (i + by) % ZN) for c in (0, ZN) for i in range(ZN)
        ]
        return shift(same, by), lax.ppermute(other, "resp", moves)

    up = terms[ZN // 2]
    for step in range(ZN // 2 - 1, 1, -1):
        up = add(shift(up, 1), terms[step])
        down = add(shift(down, -1), terms[ZN - step], HALF_ROWS if step == ZN // 2 - 1 else 0)
    up, up_got = last(shift(up, 1), terms[1], 1)
    down, down_got = last(shift(down, -1), terms[ZN - 1], -1)
    near_got = swap(near)
    dq_got = swap(dq_pair)
    dqp_out, dq_all = call(
        rows_kernel, "svvv",
        [shape((1, ROWS, HEADS * HD), BF16), shape((1, RESPS, ROWS, HEADS * HD), BF16)],
        name="rows",
    )(lengths, dqp, dq_own, dq_got)
    prefix_out = shape((1, ROWS, HD), F32)
    resp_out = shape((1, RESPS, ROWS, HD), F32)
    dkp, dvp, dkr, dvr = call(
        sums_kernel, "s" + "v" * 7, [prefix_out, prefix_out, resp_out, resp_out],
        name="sums",
    )(lengths, total, terms[0], up, down, near_got, up_got, down_got)
    return dqp_out, dq_all, dkp, dvp, dkr, dvr


def solution(mesh):
    rows = P("prompt", "resp", None)
    resp_rows = P("prompt", None, "resp", None)
    return jax.shard_map(
        per_device,
        mesh=mesh,
        in_specs=(
            rows, resp_rows, rows, rows, resp_rows, resp_rows, rows, resp_rows, P("prompt", None),
        ),
        out_specs=(rows, resp_rows, rows, rows, resp_rows, resp_rows),
        check_vma=False,
    )
```
